512 devices in a mesh: mp: 64 (over z, y), replica: 8 (over x, core).
Axes of the slice: x: 4, y: 8, z: 8, core: 2. Of those that a mesh axis runs over, the one named last changes fastest.
Arguments:
- table: float32 [32768, 256], P('mp'), may hold values from -6 to 6
- accum: float32 [32768], P('mp'), may hold values from 2 to 400
- bag_blocks: int32 [8, 4096, 3], P('replica', 'mp'), may hold values from 0 to 3
- bag_entries: int32 [8, 524288, 4], P('replica', 'mp'), may hold values from 0 to 383, as said below
- bag_weights: float32 [8, 524288, 4], P('replica', 'mp'), may hold values from 0.5 to 1.5
- bag_target: int32 [8, 524288], P('replica', 'mp'), may hold values from 0 to 511
- other_feats: bfloat16 [8, 32768, 256], P('replica', 'mp'), may hold values from -6 to 6
- cross_w: bfloat16 [2, 512, 512], replicated, may hold values from -0.25 to 0.25
- cross_b: float32 [2, 512], replicated, may hold values from -3 to 3
- evict_grads: bfloat16 [8, 2560, 128, 256], P('replica', 'mp'), may hold values from -6 to 6
- evict_owner: int32 [8, 2560, 1], P('replica', 'mp'), may hold values from 0 to 63; in each aligned block of 40 rows (0 to 39, 40 to 79, ..., all dimensions but the last counted through in order) at most 2 rows name the same one
- evict_block: int32 [8, 2560], P('replica', 'mp'), may hold values from 0 to 3
Outputs:
- cross_out: bfloat16 [8, 32768, 512], P('replica', 'mp')
- new_table: float32 [32768, 256], P('mp')
- new_accum: float32 [32768], P('mp')
The draws below stay inside these ranges and needn't reach their ends.
Inputs may be any that keep to these rules, and one draw needn't show every extreme that they name: `bag_entries`: within one row the 4 entries are distinct: entry l lies in [l * 3 * 32, (l + 1) * 3 * 32). `evict_owner`: the 40 evicted blocks of one device name one owner at most 2 times.
All inputs are finite; a program needn't handle non-finite values.
Results may differ from the reference program's by a relative error of at most 0.011.
Values may be sent and summed in bfloat16 or wider, within the bound.
No kernel may reach another device: no remote copies, remote signals or barrier semaphores. Data moves between devices by JAX's collectives and lax.ppermute only.
A program may use at most 128 MiB of HBM per device.

```python
import math
import jax
import jax.numpy as jnp
import numpy as np
from jax import lax

E = 256
BLK = 128
VB = 4
NB = 3
L = 4
CAP = 2
LAYERS = 2
B_DEV = 512
CAPP = 128
ROWS_OWN = 8192
NTILE = 64
EVICT = 40
V = 32768
D = 512
N_MP = 64
N_REPLICA = 8


def draw_bag_entries(key, part):
    key = jax.random.fold_in(key, 7)
    span = NB * BLK // L
    base = jax.random.randint(key, (N_REPLICA, N_MP * ROWS_OWN, L), 0, span, dtype=jnp.int32)
    return base + span * jnp.arange(L, dtype=jnp.int32)


def plant(values, own_key, least, top_value):
    dims = values.shape
    place = [jax.random.randint(jax.random.fold_in(own_key, axis), (), 0, dims[axis]) for axis in range(len(dims))]
    values = values.at[tuple(place)].set(least)
    longest = dims.index(max(dims))
    place[longest] = (place[longest] + 1) % dims[longest]
    return values.at[tuple(place)].set(top_value)


def level_of(key, dims, cuts, low, largest):
    level = 1.0
    for dim, blocks in cuts:
        heights = jax.random.uniform(jax.random.fold_in(jax.random.fold_in(key, 6), dim), (blocks,), jnp.float32, low / len(cuts), largest / len(cuts))
        level = level * jnp.repeat(jnp.exp(heights), dims[dim] // blocks).reshape((-1,) + (1,) * (len(dims) - 1 - dim))
    return level


def shared_out(rng, own, number, rows, number_of, top, bound, lean):
    ranking = jax.random.permutation(rng, number_of)
    crowded, ordinary = portions_of(number_of, rows * top, bound, lean, True), portions_of(number_of, rows * top, bound, lean, False)
    places = jnp.arange(number_of)

    def named(sizes, turn):
        used = int((sizes > 0).sum())
        fixed = max(1, used // 4)
        passed = fixed + (places - fixed + turn * (used - fixed)) % max(1, number_of - fixed)
        return jnp.zeros((number_of,), jnp.int32).at[ranking[jnp.where(places < fixed, places, passed)]].set(jnp.asarray(sizes, jnp.int32))

    sizes = jnp.where(number % 4 == 0, named(crowded, number // 4), named(ordinary, number - number // 4 - 1))
    mixed = jax.random.permutation(jax.random.fold_in(own, 3), number_of)
    source_of, sink = mixed[0:number_of // 2 * 2:2], mixed[1:number_of // 2 * 2:2]
    room = jnp.minimum(sizes[source_of] - 1, bound - sizes[sink]) // 2
    room = jnp.where((source_of == ranking[0]) | (sink == ranking[0]) | (sizes[sink] == 0), 0, jnp.maximum(room, 0))
    passed = jax.random.randint(jax.random.fold_in(own, 4), (number_of // 2,), 0, 1 << 20) % (room + 1)
    sizes = sizes.at[source_of].add(-passed).at[sink].add(passed)
    members = jnp.searchsorted(jnp.cumsum(sizes), jnp.arange(rows * top), side="right").astype(jnp.int32)
    listing = members.reshape(top, rows).T
    listing = listing[jax.random.permutation(jax.random.fold_in(own, 1), rows)]
    turn = jax.random.randint(jax.random.fold_in(own, 2), (rows, 1), 0, top)
    return jnp.take_along_axis(listing, (jnp.arange(top)[None, :] + turn) % top, axis=1)


def portions_of(count, total, reach, skew, full):
    loads = [(1 << 20) // math.isqrt(standing ** skew) + 1 for standing in range(1, count + 1)]
    largest = reach if full else min(reach, max(-(-total // count), total * loads[0] // sum(loads)))
    least = 1 if total - largest >= count - 1 else 0
    given, surplus = [largest] + [least] * (count - 1), total - largest - least * (count - 1)
    while surplus > 0:
        candidates = [i for i in range(1, count) if given[i] < largest] or [i for i in range(1, count) if given[i] < reach]
        pool, remaining = sum([loads[i] for i in candidates]), surplus
        for i in candidates:
            extra = min(reach - given[i], max(1, remaining * loads[i] // pool), surplus)
            given[i] = given[i] + extra
            surplus = surplus - extra
    return np.array(given)


def normal_values(stream_key, dims, deviation, limit, split=(), kind=jnp.bfloat16):
    level = level_of(stream_key, dims, split, -0.22, 0.18) if split else 1.0
    values = jax.random.normal(stream_key, dims, jnp.float32) * deviation * level
    return jnp.minimum(jnp.maximum(values, -limit), limit).astype(kind)


def setup_inputs(seed: int = 0) -> dict:
    streams_of = jax.random.split(jax.random.key(seed), 13)
    table = normal_values(streams_of[0], (V, E), 1.0, 6.0, ((0, 64),), jnp.float32)
    accum = jnp.clip(jnp.exp(math.log(400.0) - 5.2983174 * jax.random.uniform(streams_of[1], (V,), jnp.float32) ** level_of(streams_of[1], (V,), ((0, 64),), -0.2, 0.2)), 2.0, 400.0)
    bag_blocks = plant(jax.random.randint(streams_of[2], (N_REPLICA, N_MP * NTILE, NB), 0, VB), jax.random.fold_in(streams_of[2], 1), 0, VB - 1).astype(jnp.int32)
    bag_entries = draw_bag_entries(jax.random.fold_in(streams_of[12], 71), 0)
    bag_weights = jnp.clip(0.5 + 1.0 * jax.random.uniform(streams_of[4], (N_REPLICA, N_MP * ROWS_OWN, L), jnp.float32) ** level_of(streams_of[4], (N_REPLICA, N_MP * ROWS_OWN, L), ((0, 8), (1, 64)), -0.2, 0.2), 0.5, 1.5)
    bag_target = plant(jax.random.randint(streams_of[5], (N_REPLICA, N_MP * ROWS_OWN), 0, B_DEV), jax.random.fold_in(streams_of[5], 1), 0, B_DEV - 1).astype(jnp.int32)
    other_feats = normal_values(streams_of[6], (N_REPLICA, N_MP * B_DEV, E), 1.0, 6.0, ((0, 8), (1, 64)))
    cross_w = normal_values(streams_of[7], (LAYERS, D, D), D ** -0.5, 0.25)
    cross_b = normal_values(streams_of[8], (LAYERS, D), 0.5, 3.0, (), jnp.float32)
    evict_grads = normal_values(streams_of[9], (N_REPLICA, N_MP * EVICT, BLK, E), 1.0, 6.0, ((0, 8), (1, 64)))
    evict_owner_keys = jax.random.split(jax.random.fold_in(streams_of[10], 1), N_REPLICA * (N_MP * EVICT) // EVICT)
    evict_owner_turns = jax.random.permutation(jax.random.fold_in(streams_of[10], 3), N_REPLICA * (N_MP * EVICT) // EVICT)
    evict_owner = jax.vmap(lambda own, number: shared_out(jax.random.fold_in(streams_of[10], 2), own, number, EVICT, N_MP, 1, CAP, 2))(evict_owner_keys, evict_owner_turns).reshape((N_REPLICA, N_MP * EVICT, 1))
    evict_block = plant(jax.random.randint(streams_of[11], (N_REPLICA, N_MP * EVICT), 0, VB), jax.random.fold_in(streams_of[11], 1), 0, VB - 1).astype(jnp.int32)
    return {"table": table, "accum": accum, "bag_blocks": bag_blocks, "bag_entries": bag_entries, "bag_weights": bag_weights, "bag_target": bag_target, "other_feats": other_feats, "cross_w": cross_w, "cross_b": cross_b, "evict_grads": evict_grads, "evict_owner": evict_owner, "evict_block": evict_block}


learn_rate = 0.3

def reference(table, accum, bag_blocks, bag_entries, bag_weights, bag_target, other_feats, cross_w, cross_b, evict_grads, evict_owner, evict_block):
    slab_rows = VB * BLK
    rounded = lax.optimization_barrier(table.astype(jnp.bfloat16)).astype(jnp.float32)

    def owner_partial(operands):
        blocks, entries, weights, owner_no = operands
        tile_of_row = (jnp.arange(entries.shape[0], dtype=jnp.int32) // BLK).astype(jnp.int32)
        chosen = blocks[tile_of_row[:, None], entries // BLK]
        row_ids = (owner_no * slab_rows + chosen * BLK + entries % BLK).astype(jnp.int32)
        values = rounded[row_ids]
        scales = lax.optimization_barrier(weights.astype(jnp.bfloat16)).astype(jnp.float32)
        return lax.optimization_barrier(jnp.sum(scales[..., None] * values, axis=1)).astype(jnp.bfloat16)

    def group_out(operands):
        blocks, entries, weights, targets, others = operands
        pieces = lax.map(owner_partial, (blocks.reshape(N_MP, NTILE, NB), entries.reshape(N_MP, ROWS_OWN, L), weights.reshape(N_MP, ROWS_OWN, L), jnp.arange(N_MP, dtype=jnp.int32)))
        destination = (jnp.arange(ROWS_OWN, dtype=jnp.int32) // CAPP).astype(jnp.int32)
        position = (destination[None, :] * B_DEV + targets.reshape(N_MP, ROWS_OWN)).astype(jnp.int32)
        pooled = jax.ops.segment_sum(pieces.reshape(N_MP * ROWS_OWN, E).astype(jnp.float32), position.reshape(-1), num_segments=N_MP * B_DEV)
        first_input = jnp.concatenate([pooled, others.astype(jnp.float32)], axis=1)
        crossed = first_input
        for layer_index in range(LAYERS):
            mixing = jnp.dot(crossed.astype(jnp.bfloat16), cross_w[layer_index], preferred_element_type=jnp.float32) + cross_b[layer_index]
            crossed = first_input * mixing + crossed
        return crossed.astype(jnp.bfloat16)
    cross_out = lax.map(group_out, (bag_blocks, bag_entries, bag_weights, bag_target, other_feats))

    def add_group(summed, operands):
        gradients, owners, blocks = operands
        block_index = (owners[:, 0] * VB + blocks).astype(jnp.int32)
        return (summed + jax.ops.segment_sum(gradients.astype(jnp.float32), block_index, num_segments=N_MP * VB), None)
    start = jnp.zeros((N_MP * VB, BLK, E), jnp.float32)
    summed, unused = lax.scan(add_group, start, (evict_grads, evict_owner, evict_block))
    table_grad = summed.reshape(V, E)
    new_accum = accum + lax.optimization_barrier(jnp.mean(table_grad * table_grad, axis=1))
    new_table = table - learn_rate * table_grad / jnp.sqrt(new_accum)[:, None]
    return (cross_out, new_table, new_accum)
```

```python
import jax
import jax.numpy as jnp
from jax import lax
from jax.experimental import pallas as pl
from jax.experimental.pallas import tpu as pltpu
from jax.sharding import PartitionSpec as P

VMEM_LIMIT = 48 * 1024 * 1024
learn_rate = 0.3
BAG_ROWS = 16
STEP = 4


def adagrad(gradient, old_accum, old_table):
    fresh_accum = old_accum + jnp.mean(gradient * gradient, axis=1)
    fresh_table = old_table - learn_rate * gradient / jnp.sqrt(fresh_accum)[:, None]
    return (fresh_table, fresh_accum)


def pack_blocks(grads, slots, parts):
    count, rows, width = grads.shape
    part = rows // parts

    def kernel(grads_ref, slots_ref, out_ref, sems):
        copies = []
        for j in range(parts):
            copies.append(
                pltpu.make_async_copy(
                    grads_ref.at[:, pl.ds(j * part, part), :],
                    out_ref.at[j, pl.ds(0, count)],
                    sems.at[2 * j],
                )
            )
            copies.append(
                pltpu.make_async_copy(slots_ref, out_ref.at[j, pl.ds(count, 1)], sems.at[2 * j + 1])
            )
        for copy in copies:
            copy.start()
        for copy in copies:
            copy.wait()

    return pl.pallas_call(
        kernel,
        out_shape=jax.ShapeDtypeStruct((parts, count + 1, part, width), grads.dtype),
        in_specs=[pl.BlockSpec(memory_space=pl.ANY)] * 2,
        out_specs=pl.BlockSpec(memory_space=pl.ANY),
        scratch_shapes=[pltpu.SemaphoreType.DMA((2 * parts,))],
        cost_estimate=pl.CostEstimate(flops=0, bytes_accessed=2 * grads.size * 2, transcendentals=0),
        name="pack_blocks",
    )(grads, slots)


def owners_payload(recv, slots, entries, weights, targets, blocks, owner_count, block_count):
    parts, extra, part, width = recv.shape
    count = extra - 1
    rows = block_count * part
    span = 96
    lanes = 128

    def kernel(slots_ref, recv_ref, entries_ref, weights_ref, targets_ref, blocks_ref, out_ref, acc_ref):
        acc_ref[...] = jnp.zeros_like(acc_ref)

        def add(n, carry):
            for j in range(parts):
                slot = slots_ref[j * count + n]
                acc_ref[slot] = acc_ref[slot] + recv_ref[j, n].astype(jnp.float32)
            return carry

        lax.fori_loop(0, count, add, 0)
        shift = lax.broadcasted_iota(jnp.int32, (entries_ref.shape[0], lanes), 0) * span

        def place(o, carry):
            for b in range(block_count):
                out_ref[o, pl.ds(b * part, part), :] = acc_ref[o * block_count + b].astype(out_ref.dtype)
            columns = pl.ds(pl.multiple_of(o * lanes, lanes), lanes)
            bag = jnp.concatenate(
                [
                    (entries_ref[:, columns] - shift).astype(jnp.float32),
                    weights_ref[:, columns],
                    (targets_ref[:, columns] - 256).astype(jnp.float32),
                    blocks_ref[o],
                    jnp.zeros((BAG_ROWS - 10, lanes), jnp.float32),
                ],
                axis=0,
            )
            out_ref[o, pl.ds(rows, BAG_ROWS), pl.ds(0, lanes)] = bag.astype(out_ref.dtype)
            out_ref[o, pl.ds(rows, BAG_ROWS), pl.ds(lanes, width - lanes)] = jnp.zeros(
                (BAG_ROWS, width - lanes), out_ref.dtype
            )
            return carry

        lax.fori_loop(0, owner_count, place, 0)

    whole = pl.BlockSpec(memory_space=pltpu.VMEM)
    return pl.pallas_call(
        kernel,
        out_shape=jax.ShapeDtypeStruct((owner_count, rows + BAG_ROWS, width), jnp.bfloat16),
        in_specs=[pl.BlockSpec(memory_space=pltpu.SMEM)] + [whole] * 5,
        out_specs=whole,
        scratch_shapes=[pltpu.VMEM((owner_count * block_count, part, width), jnp.float32)],
        compiler_params=pltpu.CompilerParams(vmem_limit_bytes=VMEM_LIMIT),
        cost_estimate=pl.CostEstimate(flops=0, bytes_accessed=10 * 1024 * 1024, transcendentals=0),
        name="owners_payload",
    )(slots, recv, entries, weights, targets, blocks)


def pool_and_cross(tile_blocks, core, own, other, received, other_feats, cross_w, cross_b, rows):
    owner_count, block_count, half, block_rows = own.shape
    samples, other_width = other_feats.shape
    width = cross_w.shape[1]
    layers = cross_w.shape[0]
    per_tile = tile_blocks.shape[0] // owner_count
    entry_count = 4
    span = per_tile * block_rows // entry_count
    lanes = block_rows

    def kernel(blocks_ref, core_ref, own_ref, other_ref, bag_ref, feats_ref, w_ref, b_ref, out_ref, acc_ref, x_ref, y_ref):
        step = pl.program_id(0)

        @pl.when(step == 0)
        def _():
            acc_ref[...] = jnp.zeros_like(acc_ref)

        position = lax.broadcasted_iota(jnp.int32, (span, lanes), 0)
        sample = lax.broadcasted_iota(jnp.int32, (samples, STEP * lanes), 0)
        partials, targets = [], []
        for t in range(STEP):
            bag = bag_ref[t].astype(jnp.float32)
            entries = bag[0:entry_count].astype(jnp.int32)
            weights = bag[entry_count : 2 * entry_count]
            targets.append(bag[2 * entry_count : 2 * entry_count + 1].astype(jnp.int32) + 256)
            incidence = jnp.concatenate(
                [
                    jnp.where(position == entries[l : l + 1], weights[l : l + 1], 0.0)
                    for l in range(entry_count)
                ],
                axis=0,
            ).astype(jnp.bfloat16)
            chosen = [blocks_ref[(step * STEP + t) * per_tile + j] for j in range(per_tile)]
            slab = jnp.concatenate(
                [
                    jnp.concatenate([own_ref[t, b] for b in chosen], axis=1),
                    jnp.concatenate([other_ref[t, b] for b in chosen], axis=1),
                ],
                axis=0,
            )
            partials.append(
                jnp.dot(slab, incidence, preferred_element_type=jnp.float32).astype(jnp.bfloat16)
            )
        selector = jnp.where(sample == jnp.concatenate(targets, axis=1), 1.0, 0.0).astype(jnp.bfloat16)
        acc_ref[...] += lax.dot_general(
            selector,
            jnp.concatenate(partials, axis=1),
            (((1,), (1,)), ((), ())),
            preferred_element_type=jnp.float32,
        )

        @pl.when(step == pl.num_programs(0) - 1)
        def _():
            low = core_ref[0] == 0
            x_ref[:, 0:half] = jnp.where(low, acc_ref[:, 0:half], acc_ref[:, half : 2 * half])
            x_ref[:, half : 2 * half] = jnp.where(low, acc_ref[:, half : 2 * half], acc_ref[:, 0:half])
            x_ref[:, 2 * half :] = feats_ref[...].astype(jnp.float32)
            y_ref[...] = x_ref[...]
            for layer in range(layers):
                mixing = (
                    jnp.dot(y_ref[...].astype(jnp.bfloat16), w_ref[layer], preferred_element_type=jnp.float32)
                    + b_ref[layer : layer + 1, :]
                )
                if layer < layers - 1:
                    y_ref[...] = x_ref[...] * mixing + y_ref[...]
                else:
                    out_ref[...] = (x_ref[...] * mixing + y_ref[...]).astype(out_ref.dtype)

    bag_block = rows // BAG_ROWS
    return pl.pallas_call(
        kernel,
        out_shape=jax.ShapeDtypeStruct((samples, width), jnp.bfloat16),
        grid_spec=pltpu.PrefetchScalarGridSpec(
            num_scalar_prefetch=2,
            grid=(owner_count // STEP,),
            in_specs=[
                pl.BlockSpec((STEP, block_count, half, block_rows), lambda i, *_: (i, 0, 0, 0)),
                pl.BlockSpec((STEP, block_count, half, block_rows), lambda i, *_: (i, 0, 0, 0)),
                pl.BlockSpec((STEP, BAG_ROWS, lanes), lambda i, *_: (i, bag_block, 0)),
                pl.BlockSpec((samples, other_width), lambda i, *_: (0, 0)),
                pl.BlockSpec((layers, width, width), lambda i, *_: (0, 0, 0)),
                pl.BlockSpec((layers, width), lambda i, *_: (0, 0)),
            ],
            out_specs=pl.BlockSpec((samples, width), lambda i, *_: (0, 0)),
            scratch_shapes=[
                pltpu.VMEM((samples, 2 * half), jnp.float32),
                pltpu.VMEM((samples, width), jnp.float32),
                pltpu.VMEM((samples, width), jnp.float32),
            ],
        ),
        compiler_params=pltpu.CompilerParams(
            dimension_semantics=("arbitrary",), vmem_limit_bytes=VMEM_LIMIT
        ),
        cost_estimate=pl.CostEstimate(
            flops=8_000_000_000, bytes_accessed=20 * 1024 * 1024, transcendentals=0
        ),
        name="pool_and_cross",
    )(tile_blocks, core, own, other, received, other_feats, cross_w, cross_b)


def local(
    table,
    accum,
    bag_blocks,
    bag_entries,
    bag_weights,
    bag_target,
    other_feats,
    cross_w,
    cross_b,
    evict_grads,
    evict_owner,
    evict_block,
):
    owner_count = lax.axis_size("mp")
    parts = lax.axis_size("replica")
    count, block_rows, width = evict_grads.shape[1:]
    slab_rows = table.shape[0]
    block_count = slab_rows // block_rows
    part = block_rows // parts
    half = width // 2
    core = lax.axis_index("replica") % 2

    with jax.named_scope("table_gather"):
        own_half = lax.dynamic_slice(table, (0, core * half), (slab_rows, half)).astype(jnp.bfloat16)
        own_half = own_half.reshape(block_count, block_rows, half).transpose(0, 2, 1)
        own = lax.all_gather(own_half, "mp", axis=0)
        other = lax.ppermute(own, "replica", [(i, i ^ 1) for i in range(parts)])

    with jax.named_scope("evicted_over_replica"):
        slots = (evict_owner[0, :, 0] * block_count + evict_block[0]).astype(jnp.bfloat16)
        slots_block = jnp.pad(slots[None, None, :], ((0, 0), (0, part - 1), (0, width - count)))
        sent = pack_blocks(evict_grads[0], slots_block, parts)
        arrived = lax.all_to_all(sent, "replica", split_axis=0, concat_axis=0, tiled=True)
        arrived_slots = arrived[:, count, 0, :count].astype(jnp.int32).reshape(-1)

    with jax.named_scope("parts_over_mp"):
        blocks_row = jnp.pad(
            bag_blocks[0].astype(jnp.float32), ((0, 0), (0, 128 - bag_blocks.shape[2]))
        )[:, None, :]
        payload = owners_payload(
            arrived,
            arrived_slots,
            bag_entries[0].T,
            bag_weights[0].T,
            bag_target,
            blocks_row,
            owner_count,
            block_count,
        )
        received = lax.all_to_all(payload, "mp", split_axis=0, concat_axis=0, tiled=True)

    rows = block_count * part
    with jax.named_scope("table_update"):
        grad_part = jnp.sum(received[:, :rows, :].astype(jnp.float32), axis=0).astype(jnp.bfloat16)
        grads = lax.all_gather(grad_part, "replica", axis=0)
        table_grad = (
            grads.reshape(parts, block_count, part, width)
            .transpose(1, 0, 2, 3)
            .reshape(slab_rows, width)
            .astype(jnp.float32)
        )
        new_table, new_accum = adagrad(table_grad, accum, table)

    with jax.named_scope("pooling"):
        tile_blocks = received[:, rows + 9, : bag_blocks.shape[2]].astype(jnp.int32).reshape(-1)
        cross_out = pool_and_cross(
            tile_blocks,
            core.reshape(1),
            own,
            other,
            received,
            other_feats[0],
            cross_w,
            cross_b,
            rows,
        )
    return (cross_out[None], new_table, new_accum)


def solution(mesh):
    in_specs = (
        P("mp", None),
        P("mp"),
        P("replica", "mp", None),
        P("replica", "mp", None),
        P("replica", "mp", None),
        P("replica", "mp"),
        P("replica", "mp", None),
        P(),
        P(),
        P("replica", "mp", None, None),
        P("replica", "mp", None),
        P("replica", "mp"),
    )
    out_specs = (P("replica", "mp", None), P("mp", None), P("mp"))
    return jax.shard_map(local, mesh=mesh, in_specs=in_specs, out_specs=out_specs, check_vma=False)
```

```python
import jax
import jax.numpy as jnp
from jax import lax
from jax.experimental import pallas as pl
from jax.experimental.pallas import tpu as pltpu
from jax.sharding import PartitionSpec as P

VMEM_LIMIT = 48 * 1024 * 1024
learn_rate = 0.3
BAG_ROWS = 16
STEP = 4


def adagrad(gradient, old_accum, old_table):
    fresh_accum = old_accum + jnp.mean(gradient * gradient, axis=1)
    fresh_table = old_table - learn_rate * gradient / jnp.sqrt(fresh_accum)[:, None]
    return (fresh_table, fresh_accum)


def pack_blocks(grads, slots, parts):
    count, rows, width = grads.shape
    part = rows // parts

    def kernel(grads_ref, slots_ref, out_ref):
        def place(n, carry):
            for j in range(parts):
                out_ref[j, n] = grads_ref[n, pl.ds(j * part, part), :]
            return carry

        lax.fori_loop(0, count, place, 0)
        for j in range(parts):
            out_ref[j, count] = slots_ref[...]

    whole = pl.BlockSpec(memory_space=pltpu.VMEM)
    return pl.pallas_call(
        kernel,
        out_shape=jax.ShapeDtypeStruct((parts, count + 1, part, width), grads.dtype),
        in_specs=[whole] * 2,
        out_specs=whole,
        compiler_params=pltpu.CompilerParams(vmem_limit_bytes=VMEM_LIMIT),
        cost_estimate=pl.CostEstimate(flops=0, bytes_accessed=2 * grads.size * 2, transcendentals=0),
        name="pack_blocks",
    )(grads, slots)


def pack_bags(entries, weights, targets, blocks):
    owner_count, _, lanes = blocks.shape
    span = 96

    def kernel(entries_ref, weights_ref, targets_ref, blocks_ref, out_ref):
        shift = lax.broadcasted_iota(jnp.int32, (entries_ref.shape[0], lanes), 0) * span

        def place(o, carry):
            columns = pl.ds(pl.multiple_of(o * lanes, lanes), lanes)
            bag = jnp.concatenate(
                [
                    (entries_ref[:, columns] - shift).astype(jnp.float32),
                    weights_ref[:, columns],
                    (targets_ref[:, columns] - 256).astype(jnp.float32),
                    blocks_ref[o],
                    jnp.zeros((BAG_ROWS - 10, lanes), jnp.float32),
                ],
                axis=0,
            )
            out_ref[o] = bag.astype(out_ref.dtype)
            return carry

        lax.fori_loop(0, owner_count, place, 0)

    whole = pl.BlockSpec(memory_space=pltpu.VMEM)
    return pl.pallas_call(
        kernel,
        out_shape=jax.ShapeDtypeStruct((owner_count, BAG_ROWS, lanes), jnp.bfloat16),
        in_specs=[whole] * 4,
        out_specs=whole,
        compiler_params=pltpu.CompilerParams(vmem_limit_bytes=VMEM_LIMIT),
        cost_estimate=pl.CostEstimate(flops=0, bytes_accessed=1024 * 1024, transcendentals=0),
        name="pack_bags",
    )(entries, weights, targets, blocks)


def add_blocks(recv, slots, owner_count, block_count):
    parts, extra, part, width = recv.shape
    count = extra - 1

    def kernel(slots_ref, recv_ref, out_ref, acc_ref):
        acc_ref[...] = jnp.zeros_like(acc_ref)

        def add(n, carry):
            for j in range(parts):
                slot = slots_ref[j * count + n]
                acc_ref[slot] = acc_ref[slot] + recv_ref[j, n].astype(jnp.float32)
            return carry

        lax.fori_loop(0, count, add, 0)

        def place(o, carry):
            for b in range(block_count):
                out_ref[o, pl.ds(b * part, part), :] = acc_ref[o * block_count + b].astype(out_ref.dtype)
            return carry

        lax.fori_loop(0, owner_count, place, 0)

    whole = pl.BlockSpec(memory_space=pltpu.VMEM)
    return pl.pallas_call(
        kernel,
        out_shape=jax.ShapeDtypeStruct((owner_count, block_count * part, width), jnp.bfloat16),
        in_specs=[pl.BlockSpec(memory_space=pltpu.SMEM), whole],
        out_specs=whole,
        scratch_shapes=[pltpu.VMEM((owner_count * block_count, part, width), jnp.float32)],
        compiler_params=pltpu.CompilerParams(vmem_limit_bytes=VMEM_LIMIT),
        cost_estimate=pl.CostEstimate(flops=0, bytes_accessed=10 * 1024 * 1024, transcendentals=0),
        name="add_blocks",
    )(slots, recv)


def pool_and_cross(tile_blocks, core, own, other, bags, other_feats, cross_w, cross_b):
    owner_count, block_count, half, block_rows = own.shape
    samples, other_width = other_feats.shape
    width = cross_w.shape[1]
    layers = cross_w.shape[0]
    per_tile = tile_blocks.shape[0] // owner_count
    entry_count = 4
    span = per_tile * block_rows // entry_count
    lanes = block_rows

    def kernel(blocks_ref, core_ref, own_ref, other_ref, bag_ref, feats_ref, w_ref, b_ref, out_ref, acc_ref, x_ref, y_ref):
        step = pl.program_id(0)

        @pl.when(step == 0)
        def _():
            acc_ref[...] = jnp.zeros_like(acc_ref)

        position = lax.broadcasted_iota(jnp.int32, (span, lanes), 0)
        sample = lax.broadcasted_iota(jnp.int32, (samples, STEP * lanes), 0)
        partials, targets = [], []
        for t in range(STEP):
            bag = bag_ref[t].astype(jnp.float32)
            entries = bag[0:entry_count].astype(jnp.int32)
            weights = bag[entry_count : 2 * entry_count]
            targets.append(bag[2 * entry_count : 2 * entry_count + 1].astype(jnp.int32) + 256)
            incidence = jnp.concatenate(
                [
                    jnp.where(position == entries[l : l + 1], weights[l : l + 1], 0.0)
                    for l in range(entry_count)
                ],
                axis=0,
            ).astype(jnp.bfloat16)
            chosen = [blocks_ref[(step * STEP + t) * per_tile + j] for j in range(per_tile)]
            slab = jnp.concatenate(
                [
                    jnp.concatenate([own_ref[t, b] for b in chosen], axis=1),
                    jnp.concatenate([other_ref[t, b] for b in chosen], axis=1),
                ],
                axis=0,
            )
            partials.append(
                jnp.dot(slab, incidence, preferred_element_type=jnp.float32).astype(jnp.bfloat16)
            )
        selector = jnp.where(sample == jnp.concatenate(targets, axis=1), 1.0, 0.0).astype(jnp.bfloat16)
        acc_ref[...] += lax.dot_general(
            selector,
            jnp.concatenate(partials, axis=1),
            (((1,), (1,)), ((), ())),
            preferred_element_type=jnp.float32,
        )

        @pl.when(step == pl.num_programs(0) - 1)
        def _():
            low = core_ref[0] == 0
            x_ref[:, 0:half] = jnp.where(low, acc_ref[:, 0:half], acc_ref[:, half : 2 * half])
            x_ref[:, half : 2 * half] = jnp.where(low, acc_ref[:, half : 2 * half], acc_ref[:, 0:half])
            x_ref[:, 2 * half :] = feats_ref[...].astype(jnp.float32)
            y_ref[...] = x_ref[...]
            for layer in range(layers):
                mixing = (
                    jnp.dot(y_ref[...].astype(jnp.bfloat16), w_ref[layer], preferred_element_type=jnp.float32)
                    + b_ref[layer : layer + 1, :]
                )
                if layer < layers - 1:
                    y_ref[...] = x_ref[...] * mixing + y_ref[...]
                else:
                    out_ref[...] = (x_ref[...] * mixing + y_ref[...]).astype(out_ref.dtype)

    return pl.pallas_call(
        kernel,
        out_shape=jax.ShapeDtypeStruct((samples, width), jnp.bfloat16),
        grid_spec=pltpu.PrefetchScalarGridSpec(
            num_scalar_prefetch=2,
            grid=(owner_count // STEP,),
            in_specs=[
                pl.BlockSpec((STEP, block_count, half, block_rows), lambda i, *_: (i, 0, 0, 0)),
                pl.BlockSpec((STEP, block_count, half, block_rows), lambda i, *_: (i, 0, 0, 0)),
                pl.BlockSpec((STEP, BAG_ROWS, lanes), lambda i, *_: (i, 0, 0)),
                pl.BlockSpec((samples, other_width), lambda i, *_: (0, 0)),
                pl.BlockSpec((layers, width, width), lambda i, *_: (0, 0, 0)),
                pl.BlockSpec((layers, width), lambda i, *_: (0, 0)),
            ],
            out_specs=pl.BlockSpec((samples, width), lambda i, *_: (0, 0)),
            scratch_shapes=[
                pltpu.VMEM((samples, 2 * half), jnp.float32),
                pltpu.VMEM((samples, width), jnp.float32),
                pltpu.VMEM((samples, width), jnp.float32),
            ],
        ),
        compiler_params=pltpu.CompilerParams(
            dimension_semantics=("arbitrary",), vmem_limit_bytes=VMEM_LIMIT
        ),
        cost_estimate=pl.CostEstimate(
            flops=8_000_000_000, bytes_accessed=20 * 1024 * 1024, transcendentals=0
        ),
        name="pool_and_cross",
    )(tile_blocks, core, own, other, bags, other_feats, cross_w, cross_b)


def local(
    table,
    accum,
    bag_blocks,
    bag_entries,
    bag_weights,
    bag_target,
    other_feats,
    cross_w,
    cross_b,
    evict_grads,
    evict_owner,
    evict_block,
):
    owner_count = lax.axis_size("mp")
    parts = lax.axis_size("replica")
    count, block_rows, width = evict_grads.shape[1:]
    slab_rows = table.shape[0]
    block_count = slab_rows // block_rows
    part = block_rows // parts
    half = width // 2
    core = lax.axis_index("replica") % 2

    with jax.named_scope("table_gather"):
        own_half = lax.dynamic_slice(table, (0, core * half), (slab_rows, half)).astype(jnp.bfloat16)
        own_half = own_half.reshape(block_count, block_rows, half).transpose(0, 2, 1)
        own = lax.all_gather(own_half, "mp", axis=0)

    with jax.named_scope("packing"):
        slots = (evict_owner[0, :, 0] * block_count + evict_block[0]).astype(jnp.bfloat16)
        slots_block = jnp.pad(slots[None, :], ((0, part - 1), (0, width - count)))
        sent = pack_blocks(evict_grads[0], slots_block, parts)
        blocks_row = jnp.pad(
            bag_blocks[0].astype(jnp.float32), ((0, 0), (0, block_rows - bag_blocks.shape[2]))
        )[:, None, :]
        bags_sent = pack_bags(bag_entries[0].T, bag_weights[0].T, bag_target, blocks_row)
        sent, bags_sent = lax.optimization_barrier((sent, bags_sent))

    with jax.named_scope("evicted_over_replica"):
        arrived = lax.all_to_all(sent, "replica", split_axis=0, concat_axis=0, tiled=True)
        arrived_slots = arrived[:, count, 0, :count].astype(jnp.int32).reshape(-1)

    with jax.named_scope("bags_over_mp"):
        bags = lax.all_to_all(bags_sent, "mp", split_axis=0, concat_axis=0, tiled=True)
        tile_blocks = bags[:, 9, : bag_blocks.shape[2]].astype(jnp.int32).reshape(-1)

    with jax.named_scope("parts_over_mp"):
        payload = add_blocks(arrived, arrived_slots, owner_count, block_count)
        payload, bags = lax.optimization_barrier((payload, bags))
        received = lax.all_to_all(payload, "mp", split_axis=0, concat_axis=0, tiled=True)
        received, own = lax.optimization_barrier((received, own))

    with jax.named_scope("table_exchange"):
        other = lax.ppermute(own, "replica", [(i, i ^ 1) for i in range(parts)])

    with jax.named_scope("table_update"):
        grad_part = jnp.sum(received.astype(jnp.float32), axis=0).astype(jnp.bfloat16)
        grads = lax.all_gather(grad_part, "replica", axis=0)
        table_grad = (
            grads.reshape(parts, block_count, part, width)
            .transpose(1, 0, 2, 3)
            .reshape(slab_rows, width)
            .astype(jnp.float32)
        )
        new_table, new_accum = adagrad(table_grad, accum, table)

    with jax.named_scope("pooling"):
        cross_out = pool_and_cross(
            tile_blocks, core.reshape(1), own, other, bags, other_feats[0], cross_w, cross_b
        )
    return (cross_out[None], new_table, new_accum)


def solution(mesh):
    in_specs = (
        P("mp", None),
        P("mp"),
        P("replica", "mp", None),
        P("replica", "mp", None),
        P("replica", "mp", None),
        P("replica", "mp"),
        P("replica", "mp", None),
        P(),
        P(),
        P("replica", "mp", None, None),
        P("replica", "mp", None),
        P("replica", "mp"),
    )
    out_specs = (P("replica", "mp", None), P("mp", None), P("mp"))
    return jax.shard_map(local, mesh=mesh, in_specs=in_specs, out_specs=out_specs, check_vma=False)
```

```python
import jax
import jax.numpy as jnp
from jax import lax
from jax.experimental import pallas as pl
from jax.experimental.pallas import tpu as pltpu
from jax.sharding import PartitionSpec as P

VMEM_LIMIT = 48 * 1024 * 1024
learn_rate = 0.3
BAG_ROWS = 16
SAMPLES = 512


def adagrad(gradient, old_accum, old_table):
    fresh_accum = old_accum + jnp.mean(gradient * gradient, axis=1)
    fresh_table = old_table - learn_rate * gradient / jnp.sqrt(fresh_accum)[:, None]
    return (fresh_table, fresh_accum)


def pack_blocks(me, grads, slots, parts):
    count, rows, width = grads.shape
    part = rows // parts

    def kernel(me_ref, grads_ref, slots_ref, *out_refs):
        starts = [pl.multiple_of((me_ref[0] ^ k) * part, part) for k in range(parts)]

        def place(n, carry):
            for k in range(parts):
                out_refs[k][n] = grads_ref[n, pl.ds(starts[k], part), :]
            return carry

        lax.fori_loop(0, count, place, 0)
        for k in range(parts):
            out_refs[k][count] = slots_ref[...]

    whole = pl.BlockSpec(memory_space=pltpu.VMEM)
    return pl.pallas_call(
        kernel,
        out_shape=[jax.ShapeDtypeStruct((count + 1, part, width), grads.dtype)] * parts,
        in_specs=[pl.BlockSpec(memory_space=pltpu.SMEM)] + [whole] * 2,
        out_specs=[whole] * parts,
        compiler_params=pltpu.CompilerParams(vmem_limit_bytes=VMEM_LIMIT),
        cost_estimate=pl.CostEstimate(flops=0, bytes_accessed=2 * grads.size * 2, transcendentals=0),
        name="pack_blocks",
    )(me, grads, slots)


def pack_bags(entries, weights, targets, blocks):
    owner_count, _, lanes = blocks.shape
    span = 96

    def kernel(entries_ref, weights_ref, targets_ref, blocks_ref, out_ref):
        shift = lax.broadcasted_iota(jnp.int32, (entries_ref.shape[0], lanes), 0) * span

        def place(o, carry):
            columns = pl.ds(pl.multiple_of(o * lanes, lanes), lanes)
            bag = jnp.concatenate(
                [
                    (entries_ref[:, columns] - shift).astype(jnp.float32),
                    weights_ref[:, columns],
                    (targets_ref[:, columns] - 256).astype(jnp.float32),
                    blocks_ref[o],
                    jnp.zeros((BAG_ROWS - 10, lanes), jnp.float32),
                ],
                axis=0,
            )
            out_ref[o] = bag.astype(out_ref.dtype)
            return carry

        lax.fori_loop(0, owner_count, place, 0)

    whole = pl.BlockSpec(memory_space=pltpu.VMEM)
    return pl.pallas_call(
        kernel,
        out_shape=jax.ShapeDtypeStruct((owner_count, BAG_ROWS, lanes), jnp.bfloat16),
        in_specs=[whole] * 4,
        out_specs=whole,
        compiler_params=pltpu.CompilerParams(vmem_limit_bytes=VMEM_LIMIT),
        cost_estimate=pl.CostEstimate(flops=0, bytes_accessed=1024 * 1024, transcendentals=0),
        name="pack_bags",
    )(entries, weights, targets, blocks)


def add_blocks(arrived, owner_count, block_count):
    parts = len(arrived)
    extra, part, width = arrived[0].shape
    count = extra - 1
    lanes = 128

    def kernel(*refs):
        recv_refs = refs[:parts]
        out_ref, acc_ref, numbers_ref, slots_ref, sem = refs[parts:]
        for k in range(parts):
            numbers_ref[pl.ds(k, 1), :] = (
                recv_refs[k][count, :, pl.ds(0, lanes)].astype(jnp.float32)[0:1].astype(jnp.int32)
            )
        copy = pltpu.make_async_copy(numbers_ref, slots_ref, sem)
        copy.start()
        acc_ref[...] = jnp.zeros_like(acc_ref)
        copy.wait()

        def add(n, carry):
            for k in range(parts):
                slot = slots_ref[k, n]
                acc_ref[slot] = acc_ref[slot] + recv_refs[k][n].astype(jnp.float32)
            return carry

        lax.fori_loop(0, count, add, 0)

        def place(o, carry):
            for b in range(block_count):
                out_ref[o, pl.ds(b * part, part), :] = acc_ref[o * block_count + b].astype(out_ref.dtype)
            return carry

        lax.fori_loop(0, owner_count, place, 0)

    whole = pl.BlockSpec(memory_space=pltpu.VMEM)
    return pl.pallas_call(
        kernel,
        out_shape=jax.ShapeDtypeStruct((owner_count, block_count * part, width), jnp.bfloat16),
        in_specs=[whole] * parts,
        out_specs=whole,
        scratch_shapes=[
            pltpu.VMEM((owner_count * block_count, part, width), jnp.float32),
            pltpu.VMEM((parts, lanes), jnp.int32),
            pltpu.SMEM((parts, lanes), jnp.int32),
            pltpu.SemaphoreType.DMA(()),
        ],
        compiler_params=pltpu.CompilerParams(vmem_limit_bytes=VMEM_LIMIT),
        cost_estimate=pl.CostEstimate(flops=0, bytes_accessed=10 * 1024 * 1024, transcendentals=0),
        name="add_blocks",
    )(*arrived)


def pool_parts(first, many, tile_blocks, me, table, bags):
    owner_count, block_count, width, lanes = table.shape
    parts = bags.shape[0]
    per_tile = tile_blocks.shape[0] // (parts * owner_count)
    entry_count = 4
    span = per_tile * lanes // entry_count
    samples = SAMPLES

    def kernel(blocks_ref, me_ref, table_ref, bag_ref, *out_refs):
        step = pl.program_id(0)
        replica = me_ref[0] ^ (step + first)
        position = lax.broadcasted_iota(jnp.int32, (span, lanes), 0)
        sample = lax.broadcasted_iota(jnp.int32, (samples, owner_count * lanes), 0)
        partials, targets = [], []
        for t in range(owner_count):
            bag = bag_ref[0, t].astype(jnp.float32)
            entries = bag[0:entry_count].astype(jnp.int32)
            weights = bag[entry_count : 2 * entry_count]
            targets.append(bag[2 * entry_count : 2 * entry_count + 1].astype(jnp.int32) + 256)
            incidence = jnp.concatenate(
                [
                    jnp.where(position == entries[l : l + 1], weights[l : l + 1], 0.0)
                    for l in range(entry_count)
                ],
                axis=0,
            ).astype(jnp.bfloat16)
            chosen = [blocks_ref[(replica * owner_count + t) * per_tile + j] for j in range(per_tile)]
            slab = jnp.concatenate([table_ref[t, b] for b in chosen], axis=1)
            partials.append(
                jnp.dot(slab, incidence, preferred_element_type=jnp.float32).astype(jnp.bfloat16)
            )
        selector = jnp.where(sample == jnp.concatenate(targets, axis=1), 1.0, 0.0).astype(jnp.bfloat16)
        pooled = lax.dot_general(
            selector,
            jnp.concatenate(partials, axis=1),
            (((1,), (1,)), ((), ())),
            preferred_element_type=jnp.float32,
        ).astype(jnp.bfloat16)
        for i in range(many):

            @pl.when(step == i)
            def _(i=i):
                out_refs[i][...] = pooled

    return pl.pallas_call(
        kernel,
        out_shape=[jax.ShapeDtypeStruct((samples, width), jnp.bfloat16)] * many,
        grid_spec=pltpu.PrefetchScalarGridSpec(
            num_scalar_prefetch=2,
            grid=(many,),
            in_specs=[
                pl.BlockSpec((owner_count, block_count, width, lanes), lambda i, *_: (0, 0, 0, 0)),
                pl.BlockSpec(
                    (1, owner_count, BAG_ROWS, lanes),
                    lambda i, blocks_ref, me_ref: (me_ref[0] ^ (i + first), 0, 0, 0),
                ),
            ],
            out_specs=[pl.BlockSpec((samples, width), lambda i, *_: (0, 0))] * many,
        ),
        compiler_params=pltpu.CompilerParams(
            dimension_semantics=("arbitrary",), vmem_limit_bytes=VMEM_LIMIT
        ),
        cost_estimate=pl.CostEstimate(
            flops=many * 1_000_000_000, bytes_accessed=5 * 1024 * 1024, transcendentals=0
        ),
        name="pool_parts",
    )(tile_blocks, me, table, bags)


def cross_layers(pooled_parts, other_feats, cross_w, cross_b):
    parts = len(pooled_parts)
    samples, width = pooled_parts[0].shape
    layers, full, _ = cross_w.shape
    tile = 128

    def kernel(*refs):
        feats_ref, w_ref, b_ref, out_ref = refs[parts:]
        pooled = refs[0][...].astype(jnp.float32)
        for j in range(1, parts):
            pooled = pooled + refs[j][...].astype(jnp.float32)
        first = jnp.concatenate([pooled, feats_ref[...].astype(jnp.float32)], axis=1)
        crossed = first
        for layer in range(layers):
            mixing = (
                jnp.dot(crossed.astype(jnp.bfloat16), w_ref[layer], preferred_element_type=jnp.float32)
                + b_ref[layer : layer + 1, :]
            )
            crossed = first * mixing + crossed
        out_ref[...] = crossed.astype(out_ref.dtype)

    return pl.pallas_call(
        kernel,
        out_shape=jax.ShapeDtypeStruct((samples, full), jnp.bfloat16),
        grid=(samples // tile,),
        in_specs=[
            *[pl.BlockSpec((tile, width), lambda i: (i, 0))] * parts,
            pl.BlockSpec((tile, full - width), lambda i: (i, 0)),
            pl.BlockSpec((layers, full, full), lambda i: (0, 0, 0)),
            pl.BlockSpec((layers, full), lambda i: (0, 0)),
        ],
        out_specs=pl.BlockSpec((tile, full), lambda i: (i, 0)),
        compiler_params=pltpu.CompilerParams(
            dimension_semantics=("arbitrary",), vmem_limit_bytes=VMEM_LIMIT
        ),
        cost_estimate=pl.CostEstimate(
            flops=2 * layers * samples * full * full, bytes_accessed=5 * 1024 * 1024, transcendentals=0
        ),
        name="cross_layers",
    )(*pooled_parts, other_feats, cross_w, cross_b)


def local(
    table,
    accum,
    bag_blocks,
    bag_entries,
    bag_weights,
    bag_target,
    other_feats,
    cross_w,
    cross_b,
    evict_grads,
    evict_owner,
    evict_block,
):
    owner_count = lax.axis_size("mp")
    parts = lax.axis_size("replica")
    count, block_rows, width = evict_grads.shape[1:]
    slab_rows = table.shape[0]
    block_count = slab_rows // block_rows
    part = block_rows // parts
    columns = owner_count // parts
    me = lax.axis_index("replica").reshape(1)

    def to_replica(arrays, first):
        return [
            lax.ppermute(array, "replica", [(r, r ^ k) for r in range(parts)]) if k else array
            for k, array in enumerate(arrays, first)
        ]

    with jax.named_scope("packing"):
        slab = table.astype(jnp.bfloat16).reshape(block_count, block_rows, width).transpose(0, 2, 1)
        slots = (evict_owner[0, :, 0] * block_count + evict_block[0]).astype(jnp.bfloat16)
        slots_block = jnp.pad(slots[None, :], ((0, part - 1), (0, width - count)))
        sent = pack_blocks(me, evict_grads[0], slots_block, parts)
        blocks_row = jnp.pad(
            bag_blocks[0].astype(jnp.float32), ((0, 0), (0, block_rows - bag_blocks.shape[2]))
        )[:, None, :]
        bags_sent = pack_bags(bag_entries[0].T, bag_weights[0].T, bag_target, blocks_row)
        sent, bags_sent, slab = lax.optimization_barrier((sent, bags_sent, slab))

    with jax.named_scope("table_gather"):
        swap = [
            ((z * columns + y) * parts + r, (r * columns + y) * parts + z)
            for z in range(parts)
            for y in range(columns)
            for r in range(parts)
        ]
        moved = lax.ppermute(slab, ("mp", "replica"), swap)
        rows_of_z = [[z * columns + y for y in range(columns)] for z in range(parts)]
        slabs = lax.all_gather(moved, "mp", axis=0, axis_index_groups=rows_of_z)

    with jax.named_scope("evicted_over_replica"):
        arrived = to_replica(sent, 0)

    with jax.named_scope("bags_over_mp"):
        bags = lax.all_to_all(bags_sent, "mp", split_axis=0, concat_axis=0, tiled=True)
        bags = lax.all_to_all(
            bags.reshape(parts, columns, BAG_ROWS, block_rows), "replica", split_axis=0, concat_axis=0, tiled=True
        )
        tile_blocks = bags[:, :, 9, : bag_blocks.shape[2]].astype(jnp.int32).reshape(-1)

    with jax.named_scope("parts_over_mp"):
        payload = add_blocks(arrived, owner_count, block_count)
        payload, bags, tile_blocks = lax.optimization_barrier((payload, bags, tile_blocks))
        received = lax.all_to_all(payload, "mp", split_axis=0, concat_axis=0, tiled=True)

    with jax.named_scope("pooling"):
        pooled = []
        for first in range(0, parts, parts // 2):
            pooled += to_replica(pool_parts(first, parts // 2, tile_blocks, me, slabs, bags), first)

    with jax.named_scope("table_update"):
        grad_part = jnp.sum(received.astype(jnp.float32), axis=0).astype(jnp.bfloat16)
        grads = lax.all_gather(grad_part, "replica", axis=0)
        table_grad = (
            grads.reshape(parts, block_count, part, width)
            .transpose(1, 0, 2, 3)
            .reshape(slab_rows, width)
            .astype(jnp.float32)
        )
        new_table, new_accum = adagrad(table_grad, accum, table)

    with jax.named_scope("cross"):
        cross_out = cross_layers(pooled, other_feats[0], cross_w, cross_b)
    return (cross_out[None], new_table, new_accum)


def solution(mesh):
    in_specs = (
        P("mp", None),
        P("mp"),
        P("replica", "mp", None),
        P("replica", "mp", None),
        P("replica", "mp", None),
        P("replica", "mp"),
        P("replica", "mp", None),
        P(),
        P(),
        P("replica", "mp", None, None),
        P("replica", "mp", None),
        P("replica", "mp"),
    )
    out_specs = (P("replica", "mp", None), P("mp", None), P("mp"))
    return jax.shard_map(local, mesh=mesh, in_specs=in_specs, out_specs=out_specs, check_vma=False)
```

```python
import jax
import jax.numpy as jnp
from jax import lax
from jax.experimental import pallas as pl
from jax.experimental.pallas import tpu as pltpu
from jax.sharding import PartitionSpec as P

VMEM_LIMIT = 48 * 1024 * 1024
learn_rate = 0.3
BAG_ROWS = 16
SAMPLES = 512


def adagrad(gradient, old_accum, old_table):
    fresh_accum = old_accum + jnp.mean(gradient * gradient, axis=1)
    fresh_table = old_table - learn_rate * gradient / jnp.sqrt(fresh_accum)[:, None]
    return (fresh_table, fresh_accum)


def pack(place, blocks, grads, owners, numbers, entries, weights, targets, parts, columns, block_count):
    count, rows, width = grads.shape
    part = rows // parts
    span = 96
    per_tile, owner_count = blocks.shape
    lanes = entries.shape[1] // owner_count
    side = width // lanes

    def kernel(
        place_ref, blocks_ref, grads_ref, owners_ref, numbers_ref, entries_ref, weights_ref, targets_ref, out_ref, row_ref
    ):
        def cut(n, carry):
            for j in range(parts):
                out_ref[j, n] = grads_ref[n, pl.ds(j * part, part), :]
            return carry

        lax.fori_loop(0, count, cut, 0)
        row_ref[...] = jnp.zeros_like(row_ref)
        row_ref[0:1, 0:count] = (owners_ref[...] * block_count + numbers_ref[...]).astype(jnp.float32)
        slots = row_ref[...].astype(out_ref.dtype)
        shift = lax.broadcasted_iota(jnp.int32, (entries_ref.shape[0], lanes), 0) * span
        lane = lax.broadcasted_iota(jnp.int32, (1, lanes), 1)

        def bags(j, carry):
            out_ref[j, count] = slots
            z = lax.rem(j - place_ref[1] + parts, parts)
            for p in range(columns):
                d = z * columns + (place_ref[2] ^ p)
                at = pl.ds(pl.multiple_of(d * lanes, lanes), lanes)
                chosen = jnp.zeros((1, lanes), jnp.int32)
                for b in range(per_tile):
                    chosen = jnp.where(lane == b, blocks_ref[b, d], chosen)
                bag = jnp.concatenate(
                    [
                        (entries_ref[:, at] - shift).astype(jnp.float32),
                        weights_ref[:, at],
                        (targets_ref[:, at] - 256).astype(jnp.float32),
                        chosen.astype(jnp.float32),
                        jnp.zeros((BAG_ROWS - 10, lanes), jnp.float32),
                    ],
                    axis=0,
                )
                out_ref[j, count + 1 + p // side, :, pl.ds(p % side * lanes, lanes)] = bag.astype(out_ref.dtype)
            return carry

        lax.fori_loop(0, parts, bags, 0)

    whole = pl.BlockSpec(memory_space=pltpu.VMEM)
    scalars = pl.BlockSpec(memory_space=pltpu.SMEM)
    return pl.pallas_call(
        kernel,
        out_shape=jax.ShapeDtypeStruct((parts, count + 1 + columns // side, part, width), grads.dtype),
        in_specs=[scalars] * 2 + [whole] * 6,
        out_specs=whole,
        scratch_shapes=[pltpu.VMEM((part, width), jnp.float32)],
        compiler_params=pltpu.CompilerParams(vmem_limit_bytes=VMEM_LIMIT),
        cost_estimate=pl.CostEstimate(flops=0, bytes_accessed=2 * grads.size * 2, transcendentals=0),
        name="pack",
    )(place, blocks, grads, owners, numbers, entries, weights, targets)


def split_bags(bags, columns):
    parts, blocks, part, width = bags.shape
    side = columns // blocks
    lanes = width // side

    def kernel(bags_ref, *out_refs):
        for p in range(columns):
            out_refs[p][...] = bags_ref[:, p // side, :, pl.ds(p % side * lanes, lanes)]

    whole = pl.BlockSpec(memory_space=pltpu.VMEM)
    return pl.pallas_call(
        kernel,
        out_shape=[jax.ShapeDtypeStruct((parts, part, lanes), bags.dtype)] * columns,
        in_specs=[whole],
        out_specs=[whole] * columns,
        cost_estimate=pl.CostEstimate(flops=0, bytes_accessed=512 * 1024, transcendentals=0),
        name="split_bags",
    )(bags)


def add_blocks(arrived, count, owner_count, block_count):
    parts, _, part, width = arrived.shape
    lanes = 128

    def kernel(recv_ref, out_ref, acc_ref, numbers_ref, slots_ref, sem):
        for k in range(parts):
            numbers_ref[pl.ds(k, 1), :] = (
                recv_ref[k, count, :, pl.ds(0, lanes)].astype(jnp.float32)[0:1].astype(jnp.int32)
            )
        copy = pltpu.make_async_copy(numbers_ref, slots_ref, sem)
        copy.start()
        acc_ref[...] = jnp.zeros_like(acc_ref)
        copy.wait()

        def add(n, carry):
            for k in range(parts):
                slot = slots_ref[k, n]
                acc_ref[slot] = acc_ref[slot] + recv_ref[k, n].astype(jnp.float32)
            return carry

        lax.fori_loop(0, count, add, 0)

        def place(o, carry):
            for b in range(block_count):
                out_ref[o, pl.ds(b * part, part), :] = acc_ref[o * block_count + b].astype(out_ref.dtype)
            return carry

        lax.fori_loop(0, owner_count, place, 0)

    whole = pl.BlockSpec(memory_space=pltpu.VMEM)
    return pl.pallas_call(
        kernel,
        out_shape=jax.ShapeDtypeStruct((owner_count, block_count * part, width), jnp.bfloat16),
        in_specs=[whole],
        out_specs=whole,
        scratch_shapes=[
            pltpu.VMEM((owner_count * block_count, part, width), jnp.float32),
            pltpu.VMEM((parts, lanes), jnp.int32),
            pltpu.SMEM((parts, lanes), jnp.int32),
            pltpu.SemaphoreType.DMA(()),
        ],
        compiler_params=pltpu.CompilerParams(vmem_limit_bytes=VMEM_LIMIT),
        cost_estimate=pl.CostEstimate(flops=0, bytes_accessed=10 * 1024 * 1024, transcendentals=0),
        name="add_blocks",
    )(arrived)


def pool_parts(first, many, place, table, bags):
    owner_count, block_count, width, lanes = table.shape
    parts = bags[0].shape[0]
    per_tile = 3
    entry_count = 4
    span = per_tile * lanes // entry_count
    samples = SAMPLES

    def kernel(place_ref, table_ref, *refs):
        bag_refs, out_refs = refs[:owner_count], refs[owner_count : owner_count + many]
        numbers_ref, blocks_ref, sem = refs[owner_count + many :]
        step = pl.program_id(0)
        replica = place_ref[0] ^ (step + first)

        @pl.when(step == 0)
        def _():
            for p in range(owner_count):
                for r in range(parts):
                    numbers_ref[pl.ds(p * parts + r, 1), :] = (
                        bag_refs[p][r].astype(jnp.float32)[2 * entry_count + 1 : 2 * entry_count + 2].astype(jnp.int32)
                    )
            copy = pltpu.make_async_copy(numbers_ref, blocks_ref, sem)
            copy.start()
            copy.wait()

        position = lax.broadcasted_iota(jnp.int32, (span, lanes), 0)
        sample = lax.broadcasted_iota(jnp.int32, (samples, owner_count * lanes), 0)
        partials, targets = [], []
        for p in range(owner_count):
            bag = bag_refs[p][replica].astype(jnp.float32)
            entries = bag[0:entry_count].astype(jnp.int32)
            weights = bag[entry_count : 2 * entry_count]
            targets.append(bag[2 * entry_count : 2 * entry_count + 1].astype(jnp.int32) + 256)
            incidence = jnp.concatenate(
                [
                    jnp.where(position == entries[l : l + 1], weights[l : l + 1], 0.0)
                    for l in range(entry_count)
                ],
                axis=0,
            ).astype(jnp.bfloat16)
            owner = place_ref[2] ^ p
            chosen = [blocks_ref[p * parts + replica, j] for j in range(per_tile)]
            slab = jnp.concatenate([table_ref[owner, b] for b in chosen], axis=1)
            partials.append(
                jnp.dot(slab, incidence, preferred_element_type=jnp.float32).astype(jnp.bfloat16)
            )
        selector = jnp.where(sample == jnp.concatenate(targets, axis=1), 1.0, 0.0).astype(jnp.bfloat16)
        pooled = lax.dot_general(
            selector,
            jnp.concatenate(partials, axis=1),
            (((1,), (1,)), ((), ())),
            preferred_element_type=jnp.float32,
        ).astype(jnp.bfloat16)
        for i in range(many):

            @pl.when(step == i)
            def _(i=i):
                out_refs[i][...] = pooled

    whole = pl.BlockSpec(memory_space=pltpu.VMEM)
    return pl.pallas_call(
        kernel,
        out_shape=[jax.ShapeDtypeStruct((samples, width), jnp.bfloat16)] * many,
        grid=(many,),
        in_specs=[pl.BlockSpec(memory_space=pltpu.SMEM), whole] + [whole] * owner_count,
        out_specs=[whole] * many,
        scratch_shapes=[
            pltpu.VMEM((owner_count * parts, lanes), jnp.int32),
            pltpu.SMEM((owner_count * parts, lanes), jnp.int32),
            pltpu.SemaphoreType.DMA(()),
        ],
        compiler_params=pltpu.CompilerParams(
            dimension_semantics=("arbitrary",), vmem_limit_bytes=VMEM_LIMIT
        ),
        cost_estimate=pl.CostEstimate(
            flops=many * 1_000_000_000, bytes_accessed=5 * 1024 * 1024, transcendentals=0
        ),
        name="pool_parts",
    )(place, table, *bags)


def cross_layers(pooled_parts, other_feats, cross_w, cross_b):
    parts = len(pooled_parts)
    samples, width = pooled_parts[0].shape
    layers, full, _ = cross_w.shape
    tile = 128

    def kernel(*refs):
        feats_ref, w_ref, b_ref, out_ref = refs[parts:]
        pooled = refs[0][...].astype(jnp.float32)
        for j in range(1, parts):
            pooled = pooled + refs[j][...].astype(jnp.float32)
        first = jnp.concatenate([pooled, feats_ref[...].astype(jnp.float32)], axis=1)
        crossed = first
        for layer in range(layers):
            mixing = (
                jnp.dot(crossed.astype(jnp.bfloat16), w_ref[layer], preferred_element_type=jnp.float32)
                + b_ref[layer : layer + 1, :]
            )
            crossed = first * mixing + crossed
        out_ref[...] = crossed.astype(out_ref.dtype)

    return pl.pallas_call(
        kernel,
        out_shape=jax.ShapeDtypeStruct((samples, full), jnp.bfloat16),
        grid=(samples // tile,),
        in_specs=[
            *[pl.BlockSpec((tile, width), lambda i: (i, 0))] * parts,
            pl.BlockSpec((tile, full - width), lambda i: (i, 0)),
            pl.BlockSpec((layers, full, full), lambda i: (0, 0, 0)),
            pl.BlockSpec((layers, full), lambda i: (0, 0)),
        ],
        out_specs=pl.BlockSpec((tile, full), lambda i: (i, 0)),
        compiler_params=pltpu.CompilerParams(
            dimension_semantics=("arbitrary",), vmem_limit_bytes=VMEM_LIMIT
        ),
        cost_estimate=pl.CostEstimate(
            flops=2 * layers * samples * full * full, bytes_accessed=5 * 1024 * 1024, transcendentals=0
        ),
        name="cross_layers",
    )(*pooled_parts, other_feats, cross_w, cross_b)


def local(
    table,
    accum,
    bag_blocks,
    bag_entries,
    bag_weights,
    bag_target,
    other_feats,
    cross_w,
    cross_b,
    evict_grads,
    evict_owner,
    evict_block,
):
    owner_count = lax.axis_size("mp")
    parts = lax.axis_size("replica")
    count, block_rows, width = evict_grads.shape[1:]
    slab_rows = table.shape[0]
    block_count = slab_rows // block_rows
    part = block_rows // parts
    columns = owner_count // parts
    position = lax.axis_index("mp")
    place = jnp.stack([lax.axis_index("replica"), position // columns, position % columns]).astype(jnp.int32)
    along_z = [
        ((z * columns + y) * parts + r, ((r - z) % parts * columns + y) * parts + r)
        for z in range(parts)
        for y in range(columns)
        for r in range(parts)
    ]
    rows_of_z = [[z * columns + y for y in range(columns)] for z in range(parts)]

    def to_replica(arrays, first):
        return [
            lax.ppermute(array, "replica", [(r, r ^ k) for r in range(parts)]) if k else array
            for k, array in enumerate(arrays, first)
        ]

    def to_column(arrays):
        return [
            lax.ppermute(array, "mp", [(row[y], row[y ^ k]) for row in rows_of_z for y in range(columns)])
            if k
            else array
            for k, array in enumerate(arrays)
        ]

    with jax.named_scope("packing"):
        slab = table.astype(jnp.bfloat16).reshape(block_count, block_rows, width).transpose(0, 2, 1)
        sent = pack(
            place,
            bag_blocks[0].T,
            evict_grads[0],
            evict_owner[:, :, 0],
            evict_block,
            bag_entries[0].T,
            bag_weights[0].T,
            bag_target,
            parts,
            columns,
            block_count,
        )
        sent, slab = lax.optimization_barrier((sent, slab))

    with jax.named_scope("table_gather"):
        moved = lax.ppermute(slab, ("mp", "replica"), along_z)
        slabs = lax.all_gather(moved, "mp", axis=0, axis_index_groups=rows_of_z)

    with jax.named_scope("over_replica"):
        arrived = lax.all_to_all(sent, "replica", split_axis=0, concat_axis=0, tiled=True)

    with jax.named_scope("parts_over_mp"):
        payload = add_blocks(arrived, count, owner_count, block_count)
        received = lax.all_to_all(payload, "mp", split_axis=0, concat_axis=0, tiled=True)

    with jax.named_scope("bags_over_mp"):
        bags = lax.ppermute(arrived[:, count + 1 :], ("mp", "replica"), along_z)
        bags, _ = lax.optimization_barrier((bags, payload))
        bags = to_column(split_bags(bags, columns))

    with jax.named_scope("pooling"):
        pooled = []
        for first in range(0, parts, parts // 2):
            pooled += to_replica(pool_parts(first, parts // 2, place, slabs, bags), first)

    with jax.named_scope("table_update"):
        grad_part = jnp.sum(received.astype(jnp.float32), axis=0).astype(jnp.bfloat16)
        grads = lax.all_gather(grad_part, "replica", axis=0)
        table_grad = (
            grads.reshape(parts, block_count, part, width)
            .transpose(1, 0, 2, 3)
            .reshape(slab_rows, width)
            .astype(jnp.float32)
        )
        new_table, new_accum = adagrad(table_grad, accum, table)

    with jax.named_scope("cross"):
        cross_out = cross_layers(pooled, other_feats[0], cross_w, cross_b)
    return (cross_out[None], new_table, new_accum)


def solution(mesh):
    in_specs = (
        P("mp", None),
        P("mp"),
        P("replica", "mp", None),
        P("replica", "mp", None),
        P("replica", "mp", None),
        P("replica", "mp"),
        P("replica", "mp", None),
        P(),
        P(),
        P("replica", "mp", None, None),
        P("replica", "mp", None),
        P("replica", "mp"),
    )
    out_specs = (P("replica", "mp", None), P("mp", None), P("mp"))
    return jax.shard_map(local, mesh=mesh, in_specs=in_specs, out_specs=out_specs, check_vma=False)
```

```python
import jax
import jax.numpy as jnp
from jax import lax
from jax.experimental import pallas as pl
from jax.experimental.pallas import tpu as pltpu
from jax.sharding import PartitionSpec as P

VMEM_LIMIT = 48 * 1024 * 1024
learn_rate = 0.3
BAG_ROWS = 16
SAMPLES = 512


def adagrad(gradient, old_accum, old_table):
    fresh_accum = old_accum + jnp.mean(gradient * gradient, axis=1)
    fresh_table = old_table - learn_rate * gradient / jnp.sqrt(fresh_accum)[:, None]
    return (fresh_table, fresh_accum)


def pack_blocks(grads, owners, numbers, parts, block_count):
    count, rows, width = grads.shape
    part = rows // parts

    def kernel(grads_ref, owners_ref, numbers_ref, out_ref, row_ref):
        def cut(n, carry):
            for j in range(parts):
                out_ref[j, n] = grads_ref[n, pl.ds(j * part, part), :]
            return carry

        lax.fori_loop(0, count, cut, 0)
        row_ref[...] = jnp.zeros_like(row_ref)
        row_ref[0:1, 0:count] = (owners_ref[...] * block_count + numbers_ref[...]).astype(jnp.float32)
        slots = row_ref[...].astype(out_ref.dtype)
        for j in range(parts):
            out_ref[j, count] = slots

    whole = pl.BlockSpec(memory_space=pltpu.VMEM)
    return pl.pallas_call(
        kernel,
        out_shape=jax.ShapeDtypeStruct((parts, count + 1, part, width), grads.dtype),
        in_specs=[whole] * 3,
        out_specs=whole,
        scratch_shapes=[pltpu.VMEM((part, width), jnp.float32)],
        compiler_params=pltpu.CompilerParams(vmem_limit_bytes=VMEM_LIMIT),
        cost_estimate=pl.CostEstimate(flops=0, bytes_accessed=2 * grads.size * 2, transcendentals=0),
        name="pack_blocks",
    )(grads, owners, numbers)


def pack_bags(place, blocks, entries, weights, targets, columns):
    per_tile, owner_count = blocks.shape
    rows = owner_count // columns
    lanes = entries.shape[1] // owner_count
    entry_count = entries.shape[0]
    span = per_tile * lanes // entry_count

    def kernel(place_ref, blocks_ref, entries_ref, weights_ref, targets_ref, *out_refs):
        shift = lax.broadcasted_iota(jnp.int32, (entry_count, lanes), 0) * span
        lane = lax.broadcasted_iota(jnp.int32, (1, lanes), 1)

        def bags(q, carry):
            for p in range(columns):
                d = (place_ref[1] ^ q) * columns + (place_ref[2] ^ p)
                at = pl.ds(pl.multiple_of(d * lanes, lanes), lanes)
                chosen = jnp.zeros((1, lanes), jnp.int32)
                for b in range(per_tile):
                    chosen = jnp.where(lane == b, blocks_ref[b, d], chosen)
                bag = jnp.concatenate(
                    [
                        (entries_ref[:, at] - shift).astype(jnp.float32),
                        weights_ref[:, at],
                        (targets_ref[:, at] - 256).astype(jnp.float32),
                        chosen.astype(jnp.float32),
                        jnp.zeros((BAG_ROWS - 2 * entry_count - 2, lanes), jnp.float32),
                    ],
                    axis=0,
                )
                out_refs[p][q] = bag.astype(jnp.bfloat16)
            return carry

        lax.fori_loop(0, rows, bags, 0)

    whole = pl.BlockSpec(memory_space=pltpu.VMEM)
    scalars = pl.BlockSpec(memory_space=pltpu.SMEM)
    return pl.pallas_call(
        kernel,
        out_shape=[jax.ShapeDtypeStruct((rows, BAG_ROWS, lanes), jnp.bfloat16)] * columns,
        in_specs=[scalars] * 2 + [whole] * 3,
        out_specs=[whole] * columns,
        compiler_params=pltpu.CompilerParams(vmem_limit_bytes=VMEM_LIMIT),
        cost_estimate=pl.CostEstimate(flops=0, bytes_accessed=1024 * 1024, transcendentals=0),
        name="pack_bags",
    )(place, blocks, entries, weights, targets)


def turn_bags(place, bags):
    columns = len(bags)
    rows, part, lanes = bags[0].shape

    def kernel(place_ref, *refs):
        for k in range(rows):
            for p in range(columns):
                refs[columns + k][p] = refs[p][place_ref[0] ^ k]

    whole = pl.BlockSpec(memory_space=pltpu.VMEM)
    return pl.pallas_call(
        kernel,
        out_shape=[jax.ShapeDtypeStruct((columns, part, lanes), bags[0].dtype)] * rows,
        in_specs=[pl.BlockSpec(memory_space=pltpu.SMEM)] + [whole] * columns,
        out_specs=[whole] * rows,
        compiler_params=pltpu.CompilerParams(vmem_limit_bytes=VMEM_LIMIT),
        cost_estimate=pl.CostEstimate(flops=0, bytes_accessed=512 * 1024, transcendentals=0),
        name="turn_bags",
    )(place, *bags)


def add_blocks(arrived, count, owner_count, block_count):
    parts, _, part, width = arrived.shape
    lanes = 128

    def kernel(recv_ref, out_ref, acc_ref, numbers_ref, slots_ref, sem):
        for k in range(parts):
            numbers_ref[pl.ds(k, 1), :] = (
                recv_ref[k, count, :, pl.ds(0, lanes)].astype(jnp.float32)[0:1].astype(jnp.int32)
            )
        copy = pltpu.make_async_copy(numbers_ref, slots_ref, sem)
        copy.start()
        acc_ref[...] = jnp.zeros_like(acc_ref)
        copy.wait()

        def add(n, carry):
            for k in range(parts):
                slot = slots_ref[k, n]
                acc_ref[slot] = acc_ref[slot] + recv_ref[k, n].astype(jnp.float32)
            return carry

        lax.fori_loop(0, count, add, 0)

        def place(o, carry):
            for b in range(block_count):
                out_ref[o, pl.ds(b * part, part), :] = acc_ref[o * block_count + b].astype(out_ref.dtype)
            return carry

        lax.fori_loop(0, owner_count, place, 0)

    whole = pl.BlockSpec(memory_space=pltpu.VMEM)
    return pl.pallas_call(
        kernel,
        out_shape=jax.ShapeDtypeStruct((owner_count, block_count * part, width), jnp.bfloat16),
        in_specs=[whole],
        out_specs=whole,
        scratch_shapes=[
            pltpu.VMEM((owner_count * block_count, part, width), jnp.float32),
            pltpu.VMEM((parts, lanes), jnp.int32),
            pltpu.SMEM((parts, lanes), jnp.int32),
            pltpu.SemaphoreType.DMA(()),
        ],
        compiler_params=pltpu.CompilerParams(vmem_limit_bytes=VMEM_LIMIT),
        cost_estimate=pl.CostEstimate(flops=0, bytes_accessed=10 * 1024 * 1024, transcendentals=0),
        name="add_blocks",
    )(arrived)


def pool_parts(place, table, bags):
    owner_count, block_count, width, lanes = table.shape
    many = len(bags)
    per_tile = 3
    entry_count = 4
    span = per_tile * lanes // entry_count
    samples = SAMPLES

    def kernel(place_ref, table_ref, *refs):
        bag_refs, out_refs = refs[:many], refs[many : 2 * many]
        bags_ref, numbers_ref, blocks_ref, sem = refs[2 * many :]
        step = pl.program_id(0)

        @pl.when(step == 0)
        def _():
            for i in range(many):
                for p in range(owner_count):
                    bag = bag_refs[i][p]
                    bags_ref[i, p] = bag
                    numbers_ref[pl.ds(i * owner_count + p, 1), :] = (
                        bag.astype(jnp.float32)[2 * entry_count + 1 : 2 * entry_count + 2].astype(jnp.int32)
                    )
            copy = pltpu.make_async_copy(numbers_ref, blocks_ref, sem)
            copy.start()
            copy.wait()

        position = lax.broadcasted_iota(jnp.int32, (span, lanes), 0)
        sample = lax.broadcasted_iota(jnp.int32, (samples, owner_count * lanes), 0)
        partials, targets = [], []
        for p in range(owner_count):
            bag = bags_ref[step, p].astype(jnp.float32)
            entries = bag[0:entry_count].astype(jnp.int32)
            weights = bag[entry_count : 2 * entry_count]
            targets.append(bag[2 * entry_count : 2 * entry_count + 1].astype(jnp.int32) + 256)
            incidence = jnp.concatenate(
                [
                    jnp.where(position == entries[l : l + 1], weights[l : l + 1], 0.0)
                    for l in range(entry_count)
                ],
                axis=0,
            ).astype(jnp.bfloat16)
            owner = place_ref[2] ^ p
            chosen = [blocks_ref[step * owner_count + p, j] for j in range(per_tile)]
            slab = jnp.concatenate([table_ref[owner, b] for b in chosen], axis=1)
            partials.append(
                jnp.dot(slab, incidence, preferred_element_type=jnp.float32).astype(jnp.bfloat16)
            )
        selector = jnp.where(sample == jnp.concatenate(targets, axis=1), 1.0, 0.0).astype(jnp.bfloat16)
        pooled = lax.dot_general(
            selector,
            jnp.concatenate(partials, axis=1),
            (((1,), (1,)), ((), ())),
            preferred_element_type=jnp.float32,
        ).astype(jnp.bfloat16)
        for i in range(many):

            @pl.when(step == i)
            def _(i=i):
                out_refs[i][...] = pooled

    whole = pl.BlockSpec(memory_space=pltpu.VMEM)
    return pl.pallas_call(
        kernel,
        out_shape=[jax.ShapeDtypeStruct((samples, width), jnp.bfloat16)] * many,
        grid=(many,),
        in_specs=[pl.BlockSpec(memory_space=pltpu.SMEM), whole] + [whole] * many,
        out_specs=[whole] * many,
        scratch_shapes=[
            pltpu.VMEM((many, owner_count, BAG_ROWS, lanes), jnp.bfloat16),
            pltpu.VMEM((many * owner_count, lanes), jnp.int32),
            pltpu.SMEM((many * owner_count, lanes), jnp.int32),
            pltpu.SemaphoreType.DMA(()),
        ],
        compiler_params=pltpu.CompilerParams(
            dimension_semantics=("arbitrary",), vmem_limit_bytes=VMEM_LIMIT
        ),
        cost_estimate=pl.CostEstimate(
            flops=many * 1_000_000_000, bytes_accessed=5 * 1024 * 1024, transcendentals=0
        ),
        name="pool_parts",
    )(place, table, *bags)


def cross_layers(pooled_parts, other_feats, cross_w, cross_b):
    parts = len(pooled_parts)
    samples, width = pooled_parts[0].shape
    layers, full, _ = cross_w.shape
    tile = 128

    def kernel(*refs):
        feats_ref, w_ref, b_ref, out_ref = refs[parts:]
        pooled = refs[0][...].astype(jnp.float32)
        for j in range(1, parts):
            pooled = pooled + refs[j][...].astype(jnp.float32)
        first = jnp.concatenate([pooled, feats_ref[...].astype(jnp.float32)], axis=1)
        crossed = first
        for layer in range(layers):
            mixing = (
                jnp.dot(crossed.astype(jnp.bfloat16), w_ref[layer], preferred_element_type=jnp.float32)
                + b_ref[layer : layer + 1, :]
            )
            crossed = first * mixing + crossed
        out_ref[...] = crossed.astype(out_ref.dtype)

    return pl.pallas_call(
        kernel,
        out_shape=jax.ShapeDtypeStruct((samples, full), jnp.bfloat16),
        grid=(samples // tile,),
        in_specs=[
            *[pl.BlockSpec((tile, width), lambda i: (i, 0))] * parts,
            pl.BlockSpec((tile, full - width), lambda i: (i, 0)),
            pl.BlockSpec((layers, full, full), lambda i: (0, 0, 0)),
            pl.BlockSpec((layers, full), lambda i: (0, 0)),
        ],
        out_specs=pl.BlockSpec((tile, full), lambda i: (i, 0)),
        compiler_params=pltpu.CompilerParams(
            dimension_semantics=("arbitrary",), vmem_limit_bytes=VMEM_LIMIT
        ),
        cost_estimate=pl.CostEstimate(
            flops=2 * layers * samples * full * full, bytes_accessed=5 * 1024 * 1024, transcendentals=0
        ),
        name="cross_layers",
    )(*pooled_parts, other_feats, cross_w, cross_b)


def local(
    table,
    accum,
    bag_blocks,
    bag_entries,
    bag_weights,
    bag_target,
    other_feats,
    cross_w,
    cross_b,
    evict_grads,
    evict_owner,
    evict_block,
):
    owner_count = lax.axis_size("mp")
    parts = lax.axis_size("replica")
    count, block_rows, width = evict_grads.shape[1:]
    slab_rows = table.shape[0]
    block_count = slab_rows // block_rows
    part = block_rows // parts
    columns = owner_count // parts
    position = lax.axis_index("mp")
    place = jnp.stack([lax.axis_index("replica"), position // columns, position % columns]).astype(jnp.int32)

    def along_z(k):
        return [
            ((z * columns + y) * parts + r, ((z ^ r ^ k) * columns + y) * parts + r)
            for z in range(parts)
            for y in range(columns)
            for r in range(parts)
        ]

    rows_of_z = [[z * columns + y for y in range(columns)] for z in range(parts)]

    def to_replica(arrays, first):
        return [
            lax.ppermute(array, "replica", [(r, r ^ k) for r in range(parts)]) if k else array
            for k, array in enumerate(arrays, first)
        ]

    def to_column(arrays):
        return [
            lax.ppermute(array, "mp", [(row[y], row[y ^ k]) for row in rows_of_z for y in range(columns)])
            if k
            else array
            for k, array in enumerate(arrays)
        ]

    with jax.named_scope("table_gather"):
        slab = lax.optimization_barrier(table).astype(jnp.bfloat16)
        slab = slab.reshape(block_count, block_rows, width).transpose(0, 2, 1)
        moved = lax.ppermute(slab, ("mp", "replica"), along_z(0))
        slabs = lax.all_gather(moved, "mp", axis=0, axis_index_groups=rows_of_z)

    with jax.named_scope("packing"):
        bags = pack_bags(place, bag_blocks[0].T, bag_entries[0].T, bag_weights[0].T, bag_target, columns)
        sent = pack_blocks(evict_grads[0], evict_owner[:, :, 0], evict_block, parts, block_count)
        sent, bags = lax.optimization_barrier((sent, bags))

    with jax.named_scope("bags_over_mp"):
        bags = turn_bags(place, to_column(bags))
        bags = [lax.ppermute(bag, ("mp", "replica"), along_z(k)) for k, bag in enumerate(bags)]

    with jax.named_scope("over_replica"):
        arrived = lax.all_to_all(sent, "replica", split_axis=0, concat_axis=0, tiled=True)

    with jax.named_scope("parts_over_mp"):
        payload = add_blocks(arrived, count, owner_count, block_count)
        payload, bags = lax.optimization_barrier((payload, bags))
        received = lax.all_to_all(payload, "mp", split_axis=0, concat_axis=0, tiled=True)

    with jax.named_scope("pooling"):
        bags = to_replica(bags, 0)
        pooled = []
        for first in range(0, parts, parts // 2):
            pooled += to_replica(pool_parts(place, slabs, bags[first : first + parts // 2]), first)

    with jax.named_scope("table_update"):
        grad_part = jnp.sum(received.astype(jnp.float32), axis=0).astype(jnp.bfloat16)
        grads = lax.all_gather(grad_part, "replica", axis=0)
        table_grad = (
            grads.reshape(parts, block_count, part, width)
            .transpose(1, 0, 2, 3)
            .reshape(slab_rows, width)
            .astype(jnp.float32)
        )
        new_table, new_accum = adagrad(table_grad, accum, table)

    with jax.named_scope("cross"):
        cross_out = cross_layers(pooled, other_feats[0], cross_w, cross_b)
    return (cross_out[None], new_table, new_accum)


def solution(mesh):
    in_specs = (
        P("mp", None),
        P("mp"),
        P("replica", "mp", None),
        P("replica", "mp", None),
        P("replica", "mp", None),
        P("replica", "mp"),
        P("replica", "mp", None),
        P(),
        P(),
        P("replica", "mp", None, None),
        P("replica", "mp", None),
        P("replica", "mp"),
    )
    out_specs = (P("replica", "mp", None), P("mp", None), P("mp"))
    return jax.shard_map(local, mesh=mesh, in_specs=in_specs, out_specs=out_specs, check_vma=False)
```

```python
import jax
import jax.numpy as jnp
from jax import lax
from jax.experimental import pallas as pl
from jax.experimental.pallas import tpu as pltpu
from jax.sharding import Mesh
from jax.sharding import PartitionSpec as P

VMEM_LIMIT = 48 * 1024 * 1024
learn_rate = 0.3
TILE = 16
SAMPLES = 512
LOWS = ("zl", "yl")
HIGHS = ("zh", "yh")
MP = ("zh", "zl", "yh", "yl")
SIDE = 4
HIGH = SIDE * SIDE
LOW = 4


def owner_of(e, u):
    return e // SIDE * 16 + u // 2 * 8 + e % SIDE * 2 + u % 2


def adagrad(gradient, old_accum, old_table):
    fresh_accum = old_accum + jnp.mean(gradient * gradient, axis=1)
    fresh_table = old_table - learn_rate * gradient / jnp.sqrt(fresh_accum)[:, None]
    return (fresh_table, fresh_accum)


def pack_bags(blocks, entries, weights, targets):
    per_tile, owner_count = blocks.shape
    lanes = entries.shape[1] // owner_count
    entry_count = entries.shape[0]
    span = per_tile * lanes // entry_count

    def kernel(blocks_ref, entries_ref, weights_ref, targets_ref, out_ref):
        shift = lax.broadcasted_iota(jnp.int32, (entry_count, lanes), 0) * span
        lane = lax.broadcasted_iota(jnp.int32, (1, lanes), 1)

        def bags(e, carry):
            for u in range(LOW):
                d = owner_of(e, u)
                at = pl.ds(pl.multiple_of(d * lanes, lanes), lanes)
                chosen = jnp.zeros((1, lanes), jnp.int32)
                for b in range(per_tile):
                    chosen = jnp.where(lane == b, blocks_ref[b, d], chosen)
                bag = jnp.concatenate(
                    [
                        (entries_ref[:, at] - shift).astype(jnp.float32),
                        weights_ref[:, at],
                        (targets_ref[:, at] - 256).astype(jnp.float32),
                        chosen.astype(jnp.float32),
                        jnp.zeros((TILE - 2 * entry_count - 2, lanes), jnp.float32),
                    ],
                    axis=0,
                )
                out_ref[e, u] = bag.astype(out_ref.dtype)
            return carry

        lax.fori_loop(0, HIGH, bags, 0)

    whole = pl.BlockSpec(memory_space=pltpu.VMEM)
    return pl.pallas_call(
        kernel,
        out_shape=jax.ShapeDtypeStruct((HIGH, LOW, TILE, lanes), jnp.bfloat16),
        in_specs=[pl.BlockSpec(memory_space=pltpu.SMEM)] + [whole] * 3,
        out_specs=whole,
        compiler_params=pltpu.CompilerParams(vmem_limit_bytes=VMEM_LIMIT),
        cost_estimate=pl.CostEstimate(flops=0, bytes_accessed=1024 * 1024, transcendentals=0),
        name="pack_bags",
    )(blocks, entries, weights, targets)


def pack_parts(grads, owners, numbers, bags, parts, block_count):
    count, rows, width = grads.shape
    lanes = bags.shape[3]
    sides = width // lanes
    pairs = count // 2
    kept = HIGH // parts

    def kernel(grads_ref, owners_ref, numbers_ref, bags_ref, out_ref, row_ref):
        def cut(i, carry):
            for g in range(rows // TILE):
                for h in range(sides):
                    at = (pl.ds(g * TILE, TILE), pl.ds(h * lanes, lanes))
                    one = grads_ref[(2 * i, *at)].astype(jnp.float32)
                    two = grads_ref[(2 * i + 1, *at)].astype(jnp.float32)
                    for s in range(2):
                        half = slice(s * TILE // 2, (s + 1) * TILE // 2)
                        out_ref[(g * sides + h) * 2 + s, i] = jnp.concatenate([one[half], two[half]], axis=0).astype(
                            out_ref.dtype
                        )
            return carry

        lax.fori_loop(0, pairs, cut, 0)
        row_ref[...] = jnp.zeros_like(row_ref)
        row_ref[0:1, 0:count] = (owners_ref[...] * block_count + numbers_ref[...]).astype(jnp.float32)
        slots = row_ref[...].astype(out_ref.dtype)
        for t in range(LOW * parts):
            out_ref[t, pairs] = slots
            for b in range(kept):
                out_ref[t, pairs + 1 + b] = bags_ref[t % parts * kept + b, t // parts]

    whole = pl.BlockSpec(memory_space=pltpu.VMEM)
    return pl.pallas_call(
        kernel,
        out_shape=jax.ShapeDtypeStruct((LOW * parts, pairs + 1 + kept, TILE, lanes), grads.dtype),
        in_specs=[whole] * 4,
        out_specs=whole,
        scratch_shapes=[pltpu.VMEM((TILE, lanes), jnp.float32)],
        compiler_params=pltpu.CompilerParams(vmem_limit_bytes=VMEM_LIMIT),
        cost_estimate=pl.CostEstimate(flops=0, bytes_accessed=2 * grads.size * 2, transcendentals=0),
        name="pack_parts",
    )(grads, owners, numbers, bags)


def add_parts(arrived, count, parts, block_count):
    sources, tiles, _, lanes = arrived.shape
    pairs = count // 2
    kept = tiles - pairs - 1
    slot_count = HIGH * LOW * block_count
    half = TILE // 2

    def kernel(recv_ref, out_ref, bags_ref, acc_ref, numbers_ref, slots_ref, sem):
        for t in range(sources):
            numbers_ref[pl.ds(t, 1), :] = recv_ref[t, pairs].astype(jnp.float32)[0:1].astype(jnp.int32)
        copy = pltpu.make_async_copy(numbers_ref, slots_ref, sem)
        copy.start()
        acc_ref[...] = jnp.zeros_like(acc_ref)
        for t in range(sources):
            u, r = t // parts, t % parts
            for b in range(kept):
                bags_ref[r, u // 2 * 2 * kept + b * 2 + u % 2] = recv_ref[t, pairs + 1 + b]
        copy.wait()

        def add(i, carry):
            for t in range(sources):
                both = recv_ref[t, i].astype(jnp.float32)
                one, two = slots_ref[t, 2 * i], slots_ref[t, 2 * i + 1]
                acc_ref[one] = acc_ref[one] + both[0:half]
                acc_ref[two] = acc_ref[two] + both[half:TILE]
            return carry

        lax.fori_loop(0, pairs, add, 0)

        def place(e, carry):
            for u in range(LOW):
                for b in range(0, block_count, 2):
                    slot = owner_of(e, u) * block_count + b
                    out_ref[e, pl.ds((u * block_count + b) * half, TILE), :] = jnp.concatenate(
                        [acc_ref[slot], acc_ref[slot + 1]], axis=0
                    ).astype(out_ref.dtype)
            return carry

        lax.fori_loop(0, HIGH, place, 0)

    whole = pl.BlockSpec(memory_space=pltpu.VMEM)
    return pl.pallas_call(
        kernel,
        out_shape=[
            jax.ShapeDtypeStruct((HIGH, LOW * block_count * half, lanes), jnp.bfloat16),
            jax.ShapeDtypeStruct((parts, LOW * kept, TILE, lanes), jnp.bfloat16),
        ],
        in_specs=[whole],
        out_specs=[whole] * 2,
        scratch_shapes=[
            pltpu.VMEM((slot_count, half, lanes), jnp.float32),
            pltpu.VMEM((sources, lanes), jnp.int32),
            pltpu.SMEM((sources, lanes), jnp.int32),
            pltpu.SemaphoreType.DMA(()),
        ],
        compiler_params=pltpu.CompilerParams(vmem_limit_bytes=VMEM_LIMIT),
        cost_estimate=pl.CostEstimate(flops=0, bytes_accessed=10 * 1024 * 1024, transcendentals=0),
        name="add_parts",
    )(arrived)


def add_sources(received, parts):
    sources, rows, lanes = received.shape
    each = rows // LOW

    def kernel(recv_ref, out_ref):
        for u in range(LOW):
            at = pl.ds(u * each, each)
            total = recv_ref[0, at, :].astype(jnp.float32)
            for e in range(1, sources):
                total = total + recv_ref[e, at, :].astype(jnp.float32)
            total = total.astype(out_ref.dtype)
            for r in range(parts):
                out_ref[u * parts + r] = total

    whole = pl.BlockSpec(memory_space=pltpu.VMEM)
    return pl.pallas_call(
        kernel,
        out_shape=jax.ShapeDtypeStruct((LOW * parts, each, lanes), jnp.bfloat16),
        in_specs=[whole],
        out_specs=whole,
        compiler_params=pltpu.CompilerParams(vmem_limit_bytes=VMEM_LIMIT),
        cost_estimate=pl.CostEstimate(flops=0, bytes_accessed=1024 * 1024, transcendentals=0),
        name="add_sources",
    )(received)


def pool_parts(first, many, place, table, bags):
    owner_count, block_count, width, lanes = table.shape
    parts = bags.shape[0]
    per_tile = 3
    entry_count = 4
    span = per_tile * lanes // entry_count
    samples = SAMPLES

    def kernel(place_ref, table_ref, bags_ref, *refs):
        out_refs = refs[:many]
        numbers_ref, blocks_ref, sem = refs[many:]
        step = pl.program_id(0)
        replica = place_ref[0] ^ (step + first)

        @pl.when(step == 0)
        def _():
            for r in range(parts):
                for p in range(owner_count):
                    numbers_ref[pl.ds(r * owner_count + p, 1), :] = (
                        bags_ref[r, p].astype(jnp.float32)[2 * entry_count + 1 : 2 * entry_count + 2].astype(jnp.int32)
                    )
            copy = pltpu.make_async_copy(numbers_ref, blocks_ref, sem)
            copy.start()
            copy.wait()

        position = lax.broadcasted_iota(jnp.int32, (span, lanes), 0)
        sample = lax.broadcasted_iota(jnp.int32, (samples, owner_count * lanes), 0)
        partials, targets = [], []
        for p in range(owner_count):
            bag = bags_ref[replica, p].astype(jnp.float32)
            entries = bag[0:entry_count].astype(jnp.int32)
            weights = bag[entry_count : 2 * entry_count]
            targets.append(bag[2 * entry_count : 2 * entry_count + 1].astype(jnp.int32) + 256)
            incidence = jnp.concatenate(
                [
                    jnp.where(position == entries[l : l + 1], weights[l : l + 1], 0.0)
                    for l in range(entry_count)
                ],
                axis=0,
            ).astype(jnp.bfloat16)
            chosen = [blocks_ref[replica * owner_count + p, j] for j in range(per_tile)]
            slab = jnp.concatenate([table_ref[p, b] for b in chosen], axis=1)
            partials.append(
                jnp.dot(slab, incidence, preferred_element_type=jnp.float32).astype(jnp.bfloat16)
            )
        selector = jnp.where(sample == jnp.concatenate(targets, axis=1), 1.0, 0.0).astype(jnp.bfloat16)
        pooled = lax.dot_general(
            selector,
            jnp.concatenate(partials, axis=1),
            (((1,), (1,)), ((), ())),
            preferred_element_type=jnp.float32,
        ).astype(jnp.bfloat16)
        for i in range(many):

            @pl.when(step == i)
            def _(i=i):
                out_refs[i][...] = pooled

    whole = pl.BlockSpec(memory_space=pltpu.VMEM)
    return pl.pallas_call(
        kernel,
        out_shape=[jax.ShapeDtypeStruct((samples, width), jnp.bfloat16)] * many,
        grid=(many,),
        in_specs=[pl.BlockSpec(memory_space=pltpu.SMEM), whole, whole],
        out_specs=[whole] * many,
        scratch_shapes=[
            pltpu.VMEM((parts * owner_count, lanes), jnp.int32),
            pltpu.SMEM((parts * owner_count, lanes), jnp.int32),
            pltpu.SemaphoreType.DMA(()),
        ],
        compiler_params=pltpu.CompilerParams(
            dimension_semantics=("arbitrary",), vmem_limit_bytes=VMEM_LIMIT
        ),
        cost_estimate=pl.CostEstimate(
            flops=many * 1_000_000_000, bytes_accessed=5 * 1024 * 1024, transcendentals=0
        ),
        name="pool_parts",
    )(place, table, bags)


def cross_layers(pooled_parts, other_feats, cross_w, cross_b):
    parts = len(pooled_parts)
    samples, width = pooled_parts[0].shape
    layers, full, _ = cross_w.shape
    tile = 128

    def kernel(*refs):
        feats_ref, w_ref, b_ref, out_ref = refs[parts:]
        pooled = refs[0][...].astype(jnp.float32)
        for j in range(1, parts):
            pooled = pooled + refs[j][...].astype(jnp.float32)
        first = jnp.concatenate([pooled, feats_ref[...].astype(jnp.float32)], axis=1)
        crossed = first
        for layer in range(layers):
            mixing = (
                jnp.dot(crossed.astype(jnp.bfloat16), w_ref[layer], preferred_element_type=jnp.float32)
                + b_ref[layer : layer + 1, :]
            )
            crossed = first * mixing + crossed
        out_ref[...] = crossed.astype(out_ref.dtype)

    return pl.pallas_call(
        kernel,
        out_shape=jax.ShapeDtypeStruct((samples, full), jnp.bfloat16),
        grid=(samples // tile,),
        in_specs=[
            *[pl.BlockSpec((tile, width), lambda i: (i, 0))] * parts,
            pl.BlockSpec((tile, full - width), lambda i: (i, 0)),
            pl.BlockSpec((layers, full, full), lambda i: (0, 0, 0)),
            pl.BlockSpec((layers, full), lambda i: (0, 0)),
        ],
        out_specs=pl.BlockSpec((tile, full), lambda i: (i, 0)),
        compiler_params=pltpu.CompilerParams(
            dimension_semantics=("arbitrary",), vmem_limit_bytes=VMEM_LIMIT
        ),
        cost_estimate=pl.CostEstimate(
            flops=2 * layers * samples * full * full, bytes_accessed=5 * 1024 * 1024, transcendentals=0
        ),
        name="cross_layers",
    )(*pooled_parts, other_feats, cross_w, cross_b)


def local(
    table,
    accum,
    bag_blocks,
    bag_entries,
    bag_weights,
    bag_target,
    other_feats,
    cross_w,
    cross_b,
    evict_grads,
    evict_owner,
    evict_block,
):
    parts = lax.axis_size("replica")
    count, block_rows, width = evict_grads.shape[1:]
    slab_rows = table.shape[0]
    block_count = slab_rows // block_rows
    place = lax.axis_index("replica").astype(jnp.int32).reshape(1)
    lows = (*LOWS, "replica")

    def to_replica(arrays, first):
        return [
            lax.ppermute(array, "replica", [(r, r ^ k) for r in range(parts)]) if k else array
            for k, array in enumerate(arrays, first)
        ]

    with jax.named_scope("table_gather"):
        slab = lax.optimization_barrier(table).astype(jnp.bfloat16)
        slab = slab.reshape(block_count, block_rows, width).transpose(0, 2, 1)
        moves = []
        for owner in range(HIGH * LOW):
            z, y = owner // 8, owner % 8
            pooler, number = z // 2 * 2 + y // 4, z % 2 * 4 + y % 4
            moves += [(owner * parts + r, (r * 8 + number) * parts + pooler) for r in range(parts)]
        moved = lax.ppermute(slab, (*MP, "replica"), moves)
        slabs = lax.all_gather(moved, ("yh", "yl"), axis=0)

    with jax.named_scope("bags_over_high"):
        bags = pack_bags(bag_blocks[0].T, bag_entries[0].T, bag_weights[0].T, bag_target)
        bags = lax.all_to_all(bags, HIGHS, split_axis=0, concat_axis=0, tiled=True)
        bags, _ = lax.optimization_barrier((bags, moved))

    with jax.named_scope("parts_over_low"):
        sent = pack_parts(evict_grads[0], evict_owner[:, :, 0], evict_block, bags, parts, block_count)
        arrived = lax.all_to_all(sent, lows, split_axis=0, concat_axis=0, tiled=True)

    with jax.named_scope("sums_over_high"):
        sums, bags = add_parts(arrived, count, parts, block_count)
        received = lax.all_to_all(sums, HIGHS, split_axis=0, concat_axis=0, tiled=True)

    with jax.named_scope("pooling"):
        pooled = []
        for first in range(0, parts, parts // 2):
            pooled += to_replica(pool_parts(first, parts // 2, place, slabs, bags), first)

    with jax.named_scope("sums_to_owners"):
        shared = add_sources(received, parts)
        pooled, _ = lax.optimization_barrier((pooled, shared))
        grads = lax.all_to_all(shared, lows, split_axis=0, concat_axis=0, tiled=True)

    with jax.named_scope("table_update"):
        half = TILE // 2
        lanes = shared.shape[2]
        table_grad = (
            grads.reshape(block_rows // TILE, width // lanes, 2, block_count, half, lanes)
            .transpose(3, 0, 2, 4, 1, 5)
            .reshape(slab_rows, width)
            .astype(jnp.float32)
        )
        new_table, new_accum = adagrad(table_grad, accum, table)

    with jax.named_scope("cross"):
        cross_out = cross_layers(pooled, other_feats[0], cross_w, cross_b)
    return (cross_out[None], new_table, new_accum)


def solution(mesh):
    parts = mesh.shape["replica"]
    fine = Mesh(mesh.devices.reshape(SIDE, 2, SIDE, 2, parts), (*MP, "replica"))
    in_specs = (
        P(MP, None),
        P(MP),
        P("replica", MP, None),
        P("replica", MP, None),
        P("replica", MP, None),
        P("replica", MP),
        P("replica", MP, None),
        P(),
        P(),
        P("replica", MP, None, None),
        P("replica", MP, None),
        P("replica", MP),
    )
    out_specs = (P("replica", MP, None), P(MP, None), P(MP))
    return jax.shard_map(local, mesh=fine, in_specs=in_specs, out_specs=out_specs, check_vma=False)
```

```python
import jax
import jax.numpy as jnp
from jax import lax
from jax.experimental import pallas as pl
from jax.experimental.pallas import tpu as pltpu
from jax.sharding import Mesh
from jax.sharding import PartitionSpec as P

VMEM_LIMIT = 48 * 1024 * 1024
learn_rate = 0.3
TILE = 16
SMALL = pl.CostEstimate(flops=1000, bytes_accessed=1000, transcendentals=0)
TAIL = 5
SAMPLES = 512
LOWS = ("yl", "replica")
HIGHS = ("z", "yh")
MP = ("z", "yh", "yl")
SIDE = 8


def adagrad(gradient, old_accum, old_table):
    fresh_accum = old_accum + jnp.mean(gradient * gradient, axis=1)
    fresh_table = old_table - learn_rate * gradient / jnp.sqrt(fresh_accum)[:, None]
    return (fresh_table, fresh_accum)


def pack_bags(blocks, entries, weights, targets):
    per_tile, owner_count = blocks.shape
    lanes = entries.shape[1] // owner_count
    entry_count = entries.shape[0]
    span = per_tile * lanes // entry_count

    def kernel(blocks_ref, entries_ref, weights_ref, targets_ref, out_ref):
        shift = lax.broadcasted_iota(jnp.int32, (entry_count, lanes), 0) * span
        lane = lax.broadcasted_iota(jnp.int32, (1, lanes), 1)

        def bags(e, carry):
            for u in range(4):
                d = 4 * e + u
                at = pl.ds(pl.multiple_of(d * lanes, lanes), lanes)
                chosen = jnp.zeros((1, lanes), jnp.int32)
                for b in range(per_tile):
                    chosen = jnp.where(lane == b, blocks_ref[b, d], chosen)
                bag = jnp.concatenate(
                    [
                        (entries_ref[:, at] - shift).astype(jnp.float32),
                        weights_ref[:, at],
                        (targets_ref[:, at] - 256).astype(jnp.float32),
                        chosen.astype(jnp.float32),
                        jnp.zeros((TILE - 2 * entry_count - 2, lanes), jnp.float32),
                    ],
                    axis=0,
                )
                out_ref[d] = bag.astype(out_ref.dtype)
            return carry

        lax.fori_loop(0, owner_count // 4, bags, 0)

    whole = pl.BlockSpec(memory_space=pltpu.VMEM)
    return pl.pallas_call(
        kernel,
        out_shape=jax.ShapeDtypeStruct((owner_count, TILE, lanes), jnp.bfloat16),
        in_specs=[pl.BlockSpec(memory_space=pltpu.SMEM)] + [whole] * 3,
        out_specs=whole,
        compiler_params=pltpu.CompilerParams(vmem_limit_bytes=VMEM_LIMIT),
        cost_estimate=SMALL,
        name="pack_bags",
    )(blocks, entries, weights, targets)


def pack_parts(grads):
    count, rows, width = grads.shape
    lanes = 128
    sides = width // lanes
    receivers = rows // TILE * sides

    def kernel(grads_ref, out_ref):
        def cut(i, carry):
            for g in range(rows // TILE):
                for h in range(sides):
                    out_ref[g * sides + h, i] = grads_ref[i, pl.ds(g * TILE, TILE), pl.ds(h * lanes, lanes)]
            return carry

        lax.fori_loop(0, TAIL, cut, 0)

    return pl.pallas_call(
        kernel,
        out_shape=jax.ShapeDtypeStruct((receivers, count + TAIL, TILE, lanes), grads.dtype),
        grid=(count // TAIL,),
        in_specs=[pl.BlockSpec((TAIL, rows, width), lambda i: (i, 0, 0))],
        out_specs=pl.BlockSpec((receivers, TAIL, TILE, lanes), lambda i: (0, i, 0, 0)),
        compiler_params=pltpu.CompilerParams(
            dimension_semantics=("arbitrary",), vmem_limit_bytes=VMEM_LIMIT
        ),
        cost_estimate=SMALL,
        name="pack_parts",
    )(grads)


def add_bags(place, packed, owners, numbers, bags, parts, block_count):
    receivers, tiles, _, lanes = packed.shape
    count = owners.shape[1]
    kept = TAIL - 1

    def kernel(place_ref, packed_ref, owners_ref, numbers_ref, bags_ref, out_ref, row_ref):
        row_ref[...] = jnp.zeros_like(row_ref)
        row_ref[0:1, 0:count] = (owners_ref[...] * block_count + numbers_ref[...]).astype(jnp.float32)
        slots = row_ref[...].astype(out_ref.dtype)
        for t in range(receivers):
            u, j = t // parts, t % parts
            z = j ^ (place_ref[2] + u)
            out_ref[t, 0] = slots
            for b in range(kept):
                out_ref[t, 1 + b] = bags_ref[z * kept + b, u]

    whole = pl.BlockSpec(memory_space=pltpu.VMEM)
    return pl.pallas_call(
        kernel,
        out_shape=jax.ShapeDtypeStruct(packed.shape, packed.dtype),
        grid=(1,),
        in_specs=[pl.BlockSpec(memory_space=pltpu.SMEM), pl.BlockSpec(memory_space=pl.ANY), whole, whole, whole],
        out_specs=pl.BlockSpec((receivers, TAIL, TILE, lanes), lambda i: (0, tiles // TAIL - 1, 0, 0)),
        scratch_shapes=[pltpu.VMEM((TILE, lanes), jnp.float32)],
        input_output_aliases={1: 0},
        compiler_params=pltpu.CompilerParams(vmem_limit_bytes=VMEM_LIMIT),
        cost_estimate=SMALL,
        name="add_bags",
    )(place, packed, owners, numbers, bags)


def add_parts(arrived, count, parts, slot_count, highs):
    sources, _, _, lanes = arrived.shape
    kept = TAIL - 1
    lows = sources // parts
    each = slot_count // highs

    def kernel(recv_ref, out_ref, bags_ref, acc_ref, numbers_ref, slots_ref, sem):
        for t in range(sources):
            numbers_ref[pl.ds(t, 1), :] = recv_ref[t, count].astype(jnp.float32)[0:1].astype(jnp.int32)
        copy = pltpu.make_async_copy(numbers_ref, slots_ref, sem)
        copy.start()
        acc_ref[...] = jnp.zeros_like(acc_ref)
        for t in range(sources):
            for b in range(kept):
                bags_ref[t % parts, b * lows + t // parts] = recv_ref[t, count + 1 + b]
        copy.wait()

        def add(i, carry):
            for t in range(sources):
                slot = slots_ref[t, i]
                acc_ref[slot] = acc_ref[slot] + recv_ref[t, i].astype(jnp.float32)
            return carry

        lax.fori_loop(0, count, add, 0)

        def place(e, carry):
            for i in range(each):
                out_ref[e, pl.ds(i * TILE, TILE), :] = acc_ref[e * each + i].astype(out_ref.dtype)
            return carry

        lax.fori_loop(0, highs, place, 0)

    whole = pl.BlockSpec(memory_space=pltpu.VMEM)
    return pl.pallas_call(
        kernel,
        out_shape=[
            jax.ShapeDtypeStruct((highs, each * TILE, lanes), jnp.bfloat16),
            jax.ShapeDtypeStruct((parts, lows * kept, TILE, lanes), jnp.bfloat16),
        ],
        in_specs=[whole],
        out_specs=[whole] * 2,
        scratch_shapes=[
            pltpu.VMEM((slot_count, TILE, lanes), jnp.float32),
            pltpu.VMEM((sources, lanes), jnp.int32),
            pltpu.SMEM((sources, lanes), jnp.int32),
            pltpu.SemaphoreType.DMA(()),
        ],
        compiler_params=pltpu.CompilerParams(vmem_limit_bytes=VMEM_LIMIT),
        cost_estimate=SMALL,
        name="add_parts",
    )(arrived)


def add_sources(received, lows, parts):
    sources, rows, lanes = received.shape
    each = rows // lows
    tile = 32

    def kernel(recv_ref, out_ref):
        for u in range(lows):
            for first in range(0, each, tile):
                at = pl.ds(u * each + first, tile)
                total = recv_ref[0, at, :].astype(jnp.float32)
                for e in range(1, sources):
                    total = total + recv_ref[e, at, :].astype(jnp.float32)
                total = total.astype(out_ref.dtype)
                for r in range(parts):
                    out_ref[u * parts + r, pl.ds(first, tile), :] = total

    whole = pl.BlockSpec(memory_space=pltpu.VMEM)
    return pl.pallas_call(
        kernel,
        out_shape=jax.ShapeDtypeStruct((lows * parts, each, lanes), jnp.bfloat16),
        in_specs=[whole],
        out_specs=whole,
        compiler_params=pltpu.CompilerParams(vmem_limit_bytes=VMEM_LIMIT),
        cost_estimate=SMALL,
        name="add_sources",
    )(received)


def pool_parts(place, table, bags):
    owner_count, block_count, width, lanes = table.shape
    parts = bags.shape[0]
    many = parts // 2
    per_tile = 3
    entry_count = 4
    span = per_tile * lanes // entry_count
    samples = SAMPLES

    def kernel(place_ref, table_ref, bags_ref, others_ref, mine_ref, numbers_ref, blocks_ref, sem):
        step = pl.program_id(0)
        replica = place_ref[0] ^ jnp.where(step < many, 2 * step + 1, 2 * (step - many))

        @pl.when(step == 0)
        def _():
            for r in range(parts):
                for p in range(owner_count):
                    numbers_ref[pl.ds(r * owner_count + p, 1), :] = (
                        bags_ref[r, p].astype(jnp.float32)[2 * entry_count + 1 : 2 * entry_count + 2].astype(jnp.int32)
                    )
            copy = pltpu.make_async_copy(numbers_ref, blocks_ref, sem)
            copy.start()
            copy.wait()

        position = lax.broadcasted_iota(jnp.int32, (span, lanes), 0)
        sample = lax.broadcasted_iota(jnp.int32, (samples, owner_count * lanes), 0)
        partials, targets = [], []
        for p in range(owner_count):
            bag = bags_ref[replica, p].astype(jnp.float32)
            entries = bag[0:entry_count].astype(jnp.int32)
            weights = bag[entry_count : 2 * entry_count]
            targets.append(bag[2 * entry_count : 2 * entry_count + 1].astype(jnp.int32) + 256)
            incidence = jnp.concatenate(
                [
                    jnp.where(position == entries[l : l + 1], weights[l : l + 1], 0.0)
                    for l in range(entry_count)
                ],
                axis=0,
            ).astype(jnp.bfloat16)
            chosen = [blocks_ref[replica * owner_count + p, j] for j in range(per_tile)]
            owner = p ^ place_ref[1]
            slab = jnp.concatenate([table_ref[owner, b] for b in chosen], axis=1)
            partials.append(
                jnp.dot(slab, incidence, preferred_element_type=jnp.float32).astype(jnp.bfloat16)
            )
        selector = jnp.where(sample == jnp.concatenate(targets, axis=1), 1.0, 0.0).astype(jnp.bfloat16)
        pooled = lax.dot_general(
            selector,
            jnp.concatenate(partials, axis=1),
            (((1,), (1,)), ((), ())),
            preferred_element_type=jnp.float32,
        )

        @pl.when(step < many)
        def _():
            others_ref[0] = pooled

        @pl.when(step >= many)
        def _():
            mine_ref[0] = pooled

    whole = pl.BlockSpec(memory_space=pltpu.VMEM)
    return pl.pallas_call(
        kernel,
        out_shape=[jax.ShapeDtypeStruct((many, samples, width), jnp.float32)] * 2,
        grid=(parts,),
        in_specs=[pl.BlockSpec(memory_space=pltpu.SMEM), whole, whole],
        out_specs=[
            pl.BlockSpec((1, samples, width), lambda i: (jnp.minimum(i, many - 1), 0, 0)),
            pl.BlockSpec((1, samples, width), lambda i: (jnp.maximum(i - many, 0), 0, 0)),
        ],
        scratch_shapes=[
            pltpu.VMEM((parts * owner_count, lanes), jnp.int32),
            pltpu.SMEM((parts * owner_count, lanes), jnp.int32),
            pltpu.SemaphoreType.DMA(()),
        ],
        compiler_params=pltpu.CompilerParams(
            dimension_semantics=("arbitrary",), vmem_limit_bytes=VMEM_LIMIT
        ),
        cost_estimate=SMALL,
        name="pool_parts",
    )(place, table, bags)


def join(mine, theirs):
    many, samples, width = mine.shape
    tile = samples // 4

    def kernel(mine_ref, theirs_ref, *out_refs):
        for i in range(many):
            out_refs[i][...] = (mine_ref[i] + theirs_ref[i]).astype(jnp.bfloat16)

    block = pl.BlockSpec((many, tile, width), lambda i: (0, i, 0))
    return pl.pallas_call(
        kernel,
        out_shape=[jax.ShapeDtypeStruct((samples, width), jnp.bfloat16)] * many,
        grid=(samples // tile,),
        in_specs=[block] * 2,
        out_specs=[pl.BlockSpec((tile, width), lambda i: (i, 0))] * many,
        compiler_params=pltpu.CompilerParams(
            dimension_semantics=("arbitrary",), vmem_limit_bytes=VMEM_LIMIT
        ),
        cost_estimate=SMALL,
        name="join",
    )(mine, theirs)


def cross_layers(pooled_parts, other_feats, cross_w, cross_b):
    parts = len(pooled_parts)
    samples, width = pooled_parts[0].shape
    layers, full, _ = cross_w.shape
    tile = 128

    def kernel(*refs):
        feats_ref, w_ref, b_ref, out_ref = refs[parts:]
        pooled = refs[0][...].astype(jnp.float32)
        for j in range(1, parts):
            pooled = pooled + refs[j][...].astype(jnp.float32)
        first = jnp.concatenate([pooled, feats_ref[...].astype(jnp.float32)], axis=1)
        crossed = first
        for layer in range(layers):
            mixing = (
                jnp.dot(crossed.astype(jnp.bfloat16), w_ref[layer], preferred_element_type=jnp.float32)
                + b_ref[layer : layer + 1, :]
            )
            crossed = first * mixing + crossed
        out_ref[...] = crossed.astype(out_ref.dtype)

    return pl.pallas_call(
        kernel,
        out_shape=jax.ShapeDtypeStruct((samples, full), jnp.bfloat16),
        grid=(samples // tile,),
        in_specs=[
            *[pl.BlockSpec((tile, width), lambda i: (i, 0))] * parts,
            pl.BlockSpec((tile, full - width), lambda i: (i, 0)),
            pl.BlockSpec((layers, full, full), lambda i: (0, 0, 0)),
            pl.BlockSpec((layers, full), lambda i: (0, 0)),
        ],
        out_specs=pl.BlockSpec((tile, full), lambda i: (i, 0)),
        compiler_params=pltpu.CompilerParams(
            dimension_semantics=("arbitrary",), vmem_limit_bytes=VMEM_LIMIT
        ),
        cost_estimate=SMALL,
        name="cross_layers",
    )(*pooled_parts, other_feats, cross_w, cross_b)


def local(
    table,
    accum,
    bag_blocks,
    bag_entries,
    bag_weights,
    bag_target,
    other_feats,
    cross_w,
    cross_b,
    evict_grads,
    evict_owner,
    evict_block,
):
    parts = lax.axis_size("replica")
    count, block_rows, width = evict_grads.shape[1:]
    slab_rows = table.shape[0]
    block_count = slab_rows // block_rows
    highs = lax.axis_size(HIGHS)
    lows = lax.axis_size("yl")
    me = lax.axis_index("replica").astype(jnp.int32)
    y = lax.axis_index(("yh", "yl")).astype(jnp.int32)
    place = jnp.stack([me, me ^ y, y - y % lows])

    def to_replica(array, k):
        return lax.ppermute(array, "replica", [(r, r ^ k) for r in range(parts)])

    with jax.named_scope("table_gather"):
        slab = lax.optimization_barrier(table).astype(jnp.bfloat16)
        slab = slab.reshape(block_count, block_rows, width).transpose(0, 2, 1)
        moves = []
        for owner in range(SIDE * SIDE):
            own_z, own_y = owner // SIDE, owner % SIDE
            for r in range(parts):
                to_z, to_y = own_y ^ own_z, own_y ^ r
                moves.append((owner * parts + r, (to_z * SIDE + to_y) * parts + (own_z ^ to_y)))
        moved = lax.ppermute(slab, (*MP, "replica"), moves)
        slabs = lax.all_gather(moved, "z", axis=0)

    with jax.named_scope("bags_over_high"):
        bags = pack_bags(bag_blocks[0].T, bag_entries[0].T, bag_weights[0].T, bag_target)
        bags, _ = lax.optimization_barrier((bags, moved))
        bags = bags.reshape(highs, lows, TILE, bags.shape[2])
        bags = lax.all_to_all(bags, HIGHS, split_axis=0, concat_axis=0, tiled=True)

    with jax.named_scope("parts_over_low"):
        packed = pack_parts(evict_grads[0])
        sent = add_bags(place, packed, evict_owner[:, :, 0], evict_block, bags, parts, block_count)
        arrived = lax.all_to_all(sent, LOWS, split_axis=0, concat_axis=0, tiled=True)

    with jax.named_scope("sums_over_high"):
        sums, bags = add_parts(arrived, count, parts, highs * lows * block_count, highs)
        received = lax.all_to_all(sums, HIGHS, split_axis=0, concat_axis=0, tiled=True)

    with jax.named_scope("pooling"):
        others, mine = pool_parts(place, slabs, bags)
        joined = join(mine, to_replica(others, 1))
        pooled = [joined[0]] + [to_replica(joined[i], 2 * i) for i in range(1, parts // 2)]

    with jax.named_scope("sums_to_owners"):
        received, _ = lax.optimization_barrier((received, others))
        shared = add_sources(received, lows, parts)
        grads = lax.all_to_all(shared, LOWS, split_axis=0, concat_axis=0, tiled=True)

    with jax.named_scope("table_update"):
        lanes = shared.shape[2]
        table_grad = (
            grads.reshape(block_rows // TILE, width // lanes, block_count, TILE, lanes)
            .transpose(2, 0, 3, 1, 4)
            .reshape(slab_rows, width)
            .astype(jnp.float32)
        )
        new_table, new_accum = adagrad(table_grad, accum, table)

    with jax.named_scope("cross"):
        cross_out = cross_layers(pooled, other_feats[0], cross_w, cross_b)
    return (cross_out[None], new_table, new_accum)


def solution(mesh):
    parts = mesh.shape["replica"]
    fine = Mesh(mesh.devices.reshape(SIDE, SIDE // 2, 2, parts), (*MP, "replica"))
    in_specs = (
        P(MP, None),
        P(MP),
        P("replica", MP, None),
        P("replica", MP, None),
        P("replica", MP, None),
        P("replica", MP),
        P("replica", MP, None),
        P(),
        P(),
        P("replica", MP, None, None),
        P("replica", MP, None),
        P("replica", MP),
    )
    out_specs = (P("replica", MP, None), P(MP, None), P(MP))
    return jax.shard_map(local, mesh=fine, in_specs=in_specs, out_specs=out_specs, check_vma=False)
```

```python
import jax
import jax.numpy as jnp
from jax import lax
from jax.experimental import pallas as pl
from jax.experimental.pallas import tpu as pltpu
from jax.sharding import Mesh
from jax.sharding import PartitionSpec as P

VMEM_LIMIT = 48 * 1024 * 1024
ALL_VMEM = 60 * 1024 * 1024
learn_rate = 0.3
TILE = 16
SMALL = pl.CostEstimate(flops=1000, bytes_accessed=1000, transcendentals=0)
TAIL = 5
SAMPLES = 512
LOWS = ("yl", "replica")
HIGHS = ("z", "yh")
MP = ("z", "yh", "yl")
SIDE = 8


def adagrad(grads, accum, table):
    sources, rows, lanes = grads.shape
    slab_rows, width = table.shape
    sides = width // lanes
    block_count = rows // TILE
    block_rows = slab_rows // block_count

    def kernel(grads_ref, accum_ref, table_ref, new_table_ref, new_accum_ref):
        block = pl.program_id(0)
        gradient = jnp.concatenate(
            [
                jnp.concatenate([grads_ref[t + h].astype(jnp.float32) for h in range(sides)], axis=1)
                for t in range(0, sources, sides)
            ],
            axis=0,
        )
        mean = jnp.sum(gradient * gradient, axis=1, keepdims=True) * (1.0 / width)
        old = jnp.broadcast_to(accum_ref[pl.ds(block, 1), :], (block_rows, lanes)).T
        fresh = old + mean
        new_accum_ref[pl.ds(block, 1), :] = fresh.T[0:1]
        root = jnp.sqrt(fresh)
        for h in range(sides):
            at = slice(h * lanes, (h + 1) * lanes)
            new_table_ref[:, at] = table_ref[:, at] - learn_rate * gradient[:, at] / root

    return pl.pallas_call(
        kernel,
        out_shape=[
            jax.ShapeDtypeStruct((slab_rows, width), jnp.float32),
            jax.ShapeDtypeStruct((block_count, lanes), jnp.float32),
        ],
        grid=(block_count,),
        in_specs=[
            pl.BlockSpec((sources, TILE, lanes), lambda i: (0, i, 0)),
            pl.BlockSpec((block_count, lanes), lambda i: (0, 0)),
            pl.BlockSpec((block_rows, width), lambda i: (i, 0)),
        ],
        out_specs=[
            pl.BlockSpec((block_rows, width), lambda i: (i, 0)),
            pl.BlockSpec((block_count, lanes), lambda i: (0, 0)),
        ],
        compiler_params=pltpu.CompilerParams(
            dimension_semantics=("arbitrary",), vmem_limit_bytes=VMEM_LIMIT
        ),
        cost_estimate=SMALL,
        name="adagrad",
    )(grads, accum, table)


def pack_bags(blocks, entries, weights, targets):
    per_tile, _, owner_count = blocks.shape
    lanes = entries.shape[1] // owner_count
    entry_count = entries.shape[0]
    span = per_tile * lanes // entry_count
    group = owner_count // 4

    def kernel(blocks_ref, entries_ref, weights_ref, targets_ref, out_ref):
        shift = lax.broadcasted_iota(jnp.int32, (entry_count, lanes), 0) * span
        lane = lax.broadcasted_iota(jnp.int32, (1, lanes), 1)

        def bags(e, carry):
            for u in range(4):
                i = 4 * e + u
                d = pl.program_id(0) * group + i
                at = pl.ds(pl.multiple_of(i * lanes, lanes), lanes)
                chosen = jnp.zeros((1, lanes), jnp.int32)
                for b in range(per_tile):
                    chosen = jnp.where(lane == b, blocks_ref[b, 0, d], chosen)
                bag = jnp.concatenate(
                    [
                        (entries_ref[:, at] - shift).astype(jnp.float32),
                        weights_ref[:, at],
                        (targets_ref[:, at] - 256).astype(jnp.float32),
                        chosen.astype(jnp.float32),
                        jnp.zeros((TILE - 2 * entry_count - 2, lanes), jnp.float32),
                    ],
                    axis=0,
                )
                out_ref[i] = bag.astype(out_ref.dtype)
            return carry

        lax.fori_loop(0, group // 4, bags, 0)

    return pl.pallas_call(
        kernel,
        out_shape=jax.ShapeDtypeStruct((owner_count, TILE, lanes), jnp.bfloat16),
        grid=(owner_count // group,),
        in_specs=[
            pl.BlockSpec(memory_space=pltpu.SMEM),
            pl.BlockSpec((entry_count, group * lanes), lambda i: (0, i)),
            pl.BlockSpec((entry_count, group * lanes), lambda i: (0, i)),
            pl.BlockSpec((1, group * lanes), lambda i: (0, i)),
        ],
        out_specs=pl.BlockSpec((group, TILE, lanes), lambda i: (i, 0, 0)),
        compiler_params=pltpu.CompilerParams(
            dimension_semantics=("arbitrary",), vmem_limit_bytes=ALL_VMEM
        ),
        cost_estimate=SMALL,
        name="pack_bags",
    )(blocks, entries, weights, targets)


def pack_parts(grads):
    count, rows, width = grads.shape
    lanes = 128
    sides = width // lanes
    receivers = rows // TILE * sides

    def kernel(grads_ref, out_ref):
        def cut(i, carry):
            for g in range(rows // TILE):
                for h in range(sides):
                    out_ref[g * sides + h, i] = grads_ref[i, pl.ds(g * TILE, TILE), pl.ds(h * lanes, lanes)]
            return carry

        lax.fori_loop(0, TAIL, cut, 0)

    return pl.pallas_call(
        kernel,
        out_shape=jax.ShapeDtypeStruct((receivers, count + TAIL, TILE, lanes), grads.dtype),
        grid=(count // TAIL,),
        in_specs=[pl.BlockSpec((TAIL, rows, width), lambda i: (i, 0, 0))],
        out_specs=pl.BlockSpec((receivers, TAIL, TILE, lanes), lambda i: (0, i, 0, 0)),
        compiler_params=pltpu.CompilerParams(
            dimension_semantics=("arbitrary",), vmem_limit_bytes=VMEM_LIMIT
        ),
        cost_estimate=SMALL,
        name="pack_parts",
    )(grads)


def add_bags(place, packed, owners, numbers, bags, parts, block_count):
    receivers, tiles, _, lanes = packed.shape
    count = owners.shape[1]
    kept = TAIL - 1

    def kernel(place_ref, packed_ref, owners_ref, numbers_ref, bags_ref, out_ref, row_ref):
        row_ref[...] = jnp.zeros_like(row_ref)
        row_ref[0:1, 0:count] = (owners_ref[...] * block_count + numbers_ref[...]).astype(jnp.float32)
        slots = row_ref[...].astype(out_ref.dtype)
        for t in range(receivers):
            u, j = t // parts, t % parts
            group = (j + parts - place_ref[1] - u) % parts
            out_ref[t, 0] = slots
            for b in range(kept):
                out_ref[t, 1 + b] = bags_ref[(2 * b + group % 2) * kept + group // 2, u]

    whole = pl.BlockSpec(memory_space=pltpu.VMEM)
    return pl.pallas_call(
        kernel,
        out_shape=jax.ShapeDtypeStruct(packed.shape, packed.dtype),
        grid=(1,),
        in_specs=[pl.BlockSpec(memory_space=pltpu.SMEM), pl.BlockSpec(memory_space=pl.ANY), whole, whole, whole],
        out_specs=pl.BlockSpec((receivers, TAIL, TILE, lanes), lambda i: (0, tiles // TAIL - 1, 0, 0)),
        scratch_shapes=[pltpu.VMEM((TILE, lanes), jnp.float32)],
        input_output_aliases={1: 0},
        compiler_params=pltpu.CompilerParams(vmem_limit_bytes=VMEM_LIMIT),
        cost_estimate=SMALL,
        name="add_bags",
    )(place, packed, owners, numbers, bags)


def add_parts(arrived, count, parts, slot_count, highs):
    sources, _, _, lanes = arrived.shape
    kept = TAIL - 1
    lows = sources // parts
    each = slot_count // highs

    def kernel(recv_ref, out_ref, bags_ref, acc_ref, numbers_ref, slots_ref, sem):
        for t in range(sources):
            numbers_ref[pl.ds(t, 1), :] = recv_ref[t, count].astype(jnp.float32)[0:1].astype(jnp.int32)
        copy = pltpu.make_async_copy(numbers_ref, slots_ref, sem)
        copy.start()
        acc_ref[...] = jnp.zeros_like(acc_ref)
        for t in range(sources):
            for b in range(kept):
                bags_ref[t % parts, b * lows + t // parts] = recv_ref[t, count + 1 + b]
        copy.wait()

        def add(i, carry):
            for t in range(sources):
                slot = slots_ref[t, i]
                acc_ref[slot] = acc_ref[slot] + recv_ref[t, i].astype(jnp.float32)
            return carry

        lax.fori_loop(0, count, add, 0)

        def place(e, carry):
            for i in range(each):
                out_ref[e, pl.ds(i * TILE, TILE), :] = acc_ref[e * each + i].astype(out_ref.dtype)
            return carry

        lax.fori_loop(0, highs, place, 0)

    whole = pl.BlockSpec(memory_space=pltpu.VMEM)
    return pl.pallas_call(
        kernel,
        out_shape=[
            jax.ShapeDtypeStruct((highs, each * TILE, lanes), jnp.bfloat16),
            jax.ShapeDtypeStruct((parts, lows * kept, TILE, lanes), jnp.bfloat16),
        ],
        in_specs=[whole],
        out_specs=[whole] * 2,
        scratch_shapes=[
            pltpu.VMEM((slot_count, TILE, lanes), jnp.float32),
            pltpu.VMEM((sources, lanes), jnp.int32),
            pltpu.SMEM((sources, lanes), jnp.int32),
            pltpu.SemaphoreType.DMA(()),
        ],
        compiler_params=pltpu.CompilerParams(vmem_limit_bytes=VMEM_LIMIT),
        cost_estimate=SMALL,
        name="add_parts",
    )(arrived)


def add_sources(received, lows, parts):
    sources, rows, lanes = received.shape
    each = rows // lows
    tile = 32

    def kernel(recv_ref, out_ref):
        for u in range(lows):
            for first in range(0, each, tile):
                at = pl.ds(u * each + first, tile)
                total = recv_ref[0, at, :].astype(jnp.float32)
                for e in range(1, sources):
                    total = total + recv_ref[e, at, :].astype(jnp.float32)
                total = total.astype(out_ref.dtype)
                for r in range(parts):
                    out_ref[u * parts + r, pl.ds(first, tile), :] = total

    whole = pl.BlockSpec(memory_space=pltpu.VMEM)
    return pl.pallas_call(
        kernel,
        out_shape=jax.ShapeDtypeStruct((lows * parts, each, lanes), jnp.bfloat16),
        in_specs=[whole],
        out_specs=whole,
        compiler_params=pltpu.CompilerParams(vmem_limit_bytes=VMEM_LIMIT),
        cost_estimate=SMALL,
        name="add_sources",
    )(received)


def pool_parts(first, kind, place, table, bags):
    owner_count, block_count, width, lanes = table.shape
    parts = bags.shape[0]
    many = parts // 2
    per_tile = 3
    entry_count = 4
    span = per_tile * lanes // entry_count
    samples = SAMPLES

    def kernel(place_ref, table_ref, bags_ref, out_ref, numbers_ref, blocks_ref, sem):
        step = pl.program_id(0)
        replica = place_ref[0] ^ (2 * step + first)

        @pl.when(step == 0)
        def _():
            for r in range(parts):
                for p in range(owner_count):
                    numbers_ref[pl.ds(r * owner_count + p, 1), :] = (
                        bags_ref[r, p].astype(jnp.float32)[2 * entry_count + 1 : 2 * entry_count + 2].astype(jnp.int32)
                    )
            copy = pltpu.make_async_copy(numbers_ref, blocks_ref, sem)
            copy.start()
            copy.wait()

        position = lax.broadcasted_iota(jnp.int32, (span, lanes), 0)
        sample = lax.broadcasted_iota(jnp.int32, (samples, owner_count * lanes), 0)
        partials, targets = [], []
        for p in range(owner_count):
            bag = bags_ref[replica, p].astype(jnp.float32)
            entries = bag[0:entry_count].astype(jnp.int32)
            weights = bag[entry_count : 2 * entry_count]
            targets.append(bag[2 * entry_count : 2 * entry_count + 1].astype(jnp.int32) + 256)
            incidence = jnp.concatenate(
                [
                    jnp.where(position == entries[l : l + 1], weights[l : l + 1], 0.0)
                    for l in range(entry_count)
                ],
                axis=0,
            ).astype(jnp.bfloat16)
            chosen = [blocks_ref[replica * owner_count + p, j] for j in range(per_tile)]
            slab = jnp.concatenate([table_ref[p, b] for b in chosen], axis=1)
            partials.append(
                jnp.dot(slab, incidence, preferred_element_type=jnp.float32).astype(jnp.bfloat16)
            )
        selector = jnp.where(sample == jnp.concatenate(targets, axis=1), 1.0, 0.0).astype(jnp.bfloat16)
        out_ref[0] = lax.dot_general(
            selector,
            jnp.concatenate(partials, axis=1),
            (((1,), (1,)), ((), ())),
            preferred_element_type=jnp.float32,
        ).astype(kind)

    whole = pl.BlockSpec(memory_space=pltpu.VMEM)
    return pl.pallas_call(
        kernel,
        out_shape=jax.ShapeDtypeStruct((many, samples, width), kind),
        grid=(many,),
        in_specs=[pl.BlockSpec(memory_space=pltpu.SMEM), whole, whole],
        out_specs=pl.BlockSpec((1, samples, width), lambda i: (i, 0, 0)),
        scratch_shapes=[
            pltpu.VMEM((parts * owner_count, lanes), jnp.int32),
            pltpu.SMEM((parts * owner_count, lanes), jnp.int32),
            pltpu.SemaphoreType.DMA(()),
        ],
        compiler_params=pltpu.CompilerParams(
            dimension_semantics=("arbitrary",), vmem_limit_bytes=VMEM_LIMIT
        ),
        cost_estimate=SMALL,
        name="pool_parts",
    )(place, table, bags)


def join(mine, theirs):
    many, samples, width = mine.shape
    tile = samples // 4

    def kernel(mine_ref, theirs_ref, *out_refs):
        for i in range(many):
            out_refs[i][...] = (mine_ref[i] + theirs_ref[i].astype(jnp.float32)).astype(jnp.bfloat16)

    block = pl.BlockSpec((many, tile, width), lambda i: (0, i, 0))
    return pl.pallas_call(
        kernel,
        out_shape=[jax.ShapeDtypeStruct((samples, width), jnp.bfloat16)] * many,
        grid=(samples // tile,),
        in_specs=[block] * 2,
        out_specs=[pl.BlockSpec((tile, width), lambda i: (i, 0))] * many,
        compiler_params=pltpu.CompilerParams(
            dimension_semantics=("arbitrary",), vmem_limit_bytes=VMEM_LIMIT
        ),
        cost_estimate=SMALL,
        name="join",
    )(mine, theirs)


def cross_layers(pooled_parts, other_feats, cross_w, cross_b):
    parts = len(pooled_parts)
    samples, width = pooled_parts[0].shape
    layers, full, _ = cross_w.shape
    tile = 128

    def kernel(*refs):
        feats_ref, w_ref, b_ref, out_ref = refs[parts:]
        pooled = refs[0][...].astype(jnp.float32)
        for j in range(1, parts):
            pooled = pooled + refs[j][...].astype(jnp.float32)
        first = jnp.concatenate([pooled, feats_ref[...].astype(jnp.float32)], axis=1)
        crossed = first
        for layer in range(layers):
            mixing = (
                jnp.dot(crossed.astype(jnp.bfloat16), w_ref[layer], preferred_element_type=jnp.float32)
                + b_ref[layer : layer + 1, :]
            )
            crossed = first * mixing + crossed
        out_ref[...] = crossed.astype(out_ref.dtype)

    return pl.pallas_call(
        kernel,
        out_shape=jax.ShapeDtypeStruct((samples, full), jnp.bfloat16),
        grid=(samples // tile,),
        in_specs=[
            *[pl.BlockSpec((tile, width), lambda i: (i, 0))] * parts,
            pl.BlockSpec((tile, full - width), lambda i: (i, 0)),
            pl.BlockSpec((layers, full, full), lambda i: (0, 0, 0)),
            pl.BlockSpec((layers, full), lambda i: (0, 0)),
        ],
        out_specs=pl.BlockSpec((tile, full), lambda i: (i, 0)),
        compiler_params=pltpu.CompilerParams(
            dimension_semantics=("arbitrary",), vmem_limit_bytes=VMEM_LIMIT
        ),
        cost_estimate=SMALL,
        name="cross_layers",
    )(*pooled_parts, other_feats, cross_w, cross_b)


def local(
    table,
    accum,
    bag_blocks,
    bag_entries,
    bag_weights,
    bag_target,
    other_feats,
    cross_w,
    cross_b,
    evict_grads,
    evict_owner,
    evict_block,
):
    parts = lax.axis_size("replica")
    count, block_rows, width = evict_grads.shape[1:]
    slab_rows = table.shape[0]
    block_count = slab_rows // block_rows
    highs = lax.axis_size(HIGHS)
    lows = lax.axis_size("yl")
    me = lax.axis_index("replica").astype(jnp.int32)
    y = lax.axis_index(("yh", "yl")).astype(jnp.int32)
    place = jnp.stack([me, y - y % lows])

    def to_replica(array, k):
        return lax.ppermute(array, "replica", [(r, r ^ k) for r in range(parts)])

    with jax.named_scope("table_gather"):
        slab = lax.optimization_barrier(table).astype(jnp.bfloat16)
        slab = slab.reshape(block_count, block_rows, width).transpose(0, 2, 1)
        moves = []
        for owner in range(SIDE * SIDE):
            z, y_own = owner // SIDE, owner % SIDE
            to_z, group = z // 2 * 2 + y_own % 2, y_own // 2 * 2 + z % 2
            moves += [(owner * parts + r, (to_z * SIDE + (r - group) % SIDE) * parts + r) for r in range(parts)]
        moved = lax.ppermute(slab, (*MP, "replica"), moves)
        slabs = lax.all_gather(moved, "z", axis=0)

    with jax.named_scope("bags_over_high"):
        bags = pack_bags(bag_blocks.transpose(2, 0, 1), bag_entries[0].T, bag_weights[0].T, bag_target)
        bags = bags.reshape(highs, lows, TILE, bags.shape[2])
        bags = lax.all_to_all(bags, HIGHS, split_axis=0, concat_axis=0, tiled=True)
        bags, _ = lax.optimization_barrier((bags, moved))

    with jax.named_scope("parts_over_low"):
        packed = pack_parts(evict_grads[0])
        sent = add_bags(place, packed, evict_owner[:, :, 0], evict_block, bags, parts, block_count)
        arrived = lax.all_to_all(sent, LOWS, split_axis=0, concat_axis=0, tiled=True)

    with jax.named_scope("sums_over_high"):
        sums, bags = add_parts(arrived, count, parts, highs * lows * block_count, highs)
        received = lax.all_to_all(sums, HIGHS, split_axis=0, concat_axis=0, tiled=True)

    with jax.named_scope("pooling"):
        others = pool_parts(1, jnp.bfloat16, place, slabs, bags)
        mine = pool_parts(0, jnp.float32, place, slabs, bags)
        joined = join(mine, to_replica(others, 1))
        pooled = [joined[0]] + [to_replica(joined[i], 2 * i) for i in (2, 3, 1)]

    with jax.named_scope("sums_to_owners"):
        received, _ = lax.optimization_barrier((received, pooled))
        shared = add_sources(received, lows, parts)
        grads = lax.all_to_all(shared, LOWS, split_axis=0, concat_axis=0, tiled=True)

    with jax.named_scope("table_update"):
        new_table, new_accum = adagrad(grads, accum.reshape(block_count, block_rows), table)
        new_accum = new_accum.reshape(slab_rows)

    with jax.named_scope("cross"):
        cross_out = cross_layers(pooled, other_feats[0], cross_w, cross_b)
    return (cross_out[None], new_table, new_accum)


def solution(mesh):
    parts = mesh.shape["replica"]
    fine = Mesh(mesh.devices.reshape(SIDE, SIDE // 2, 2, parts), (*MP, "replica"))
    in_specs = (
        P(MP, None),
        P(MP),
        P("replica", MP, None),
        P("replica", MP, None),
        P("replica", MP, None),
        P("replica", MP),
        P("replica", MP, None),
        P(),
        P(),
        P("replica", MP, None, None),
        P("replica", MP, None),
        P("replica", MP),
    )
    out_specs = (P("replica", MP, None), P(MP, None), P(MP))
    return jax.shard_map(local, mesh=fine, in_specs=in_specs, out_specs=out_specs, check_vma=False)
```

```python
import jax
import jax.numpy as jnp
from jax import lax
from jax.experimental import pallas as pl
from jax.experimental.pallas import tpu as pltpu
from jax.sharding import Mesh
from jax.sharding import PartitionSpec as P

VMEM_LIMIT = 48 * 1024 * 1024
ALL_VMEM = 60 * 1024 * 1024
learn_rate = 0.3
TILE = 16
SMALL = pl.CostEstimate(flops=1000, bytes_accessed=1000, transcendentals=0)
TAIL = 5
SAMPLES = 512
LOWS = ("yl", "replica")
HIGHS = ("z", "yh")
MP = ("z", "yh", "yl")
SIDE = 8


def adagrad(grads, accum, table):
    sources, rows, lanes = grads.shape
    slab_rows, width = table.shape
    sides = width // lanes
    block_count = rows // TILE
    block_rows = slab_rows // block_count

    def kernel(grads_ref, accum_ref, table_ref, new_table_ref, new_accum_ref):
        block = pl.program_id(0)
        gradient = jnp.concatenate(
            [
                jnp.concatenate([grads_ref[t + h].astype(jnp.float32) for h in range(sides)], axis=1)
                for t in range(0, sources, sides)
            ],
            axis=0,
        )
        mean = jnp.sum(gradient * gradient, axis=1, keepdims=True) * (1.0 / width)
        old = jnp.broadcast_to(accum_ref[pl.ds(block, 1), :], (block_rows, lanes)).T
        fresh = old + mean
        new_accum_ref[pl.ds(block, 1), :] = fresh.T[0:1]
        root = jnp.sqrt(fresh)
        for h in range(sides):
            at = slice(h * lanes, (h + 1) * lanes)
            new_table_ref[:, at] = table_ref[:, at] - learn_rate * gradient[:, at] / root

    return pl.pallas_call(
        kernel,
        out_shape=[
            jax.ShapeDtypeStruct((slab_rows, width), jnp.float32),
            jax.ShapeDtypeStruct((block_count, lanes), jnp.float32),
        ],
        grid=(block_count,),
        in_specs=[
            pl.BlockSpec((sources, TILE, lanes), lambda i: (0, i, 0)),
            pl.BlockSpec((block_count, lanes), lambda i: (0, 0)),
            pl.BlockSpec((block_rows, width), lambda i: (i, 0)),
        ],
        out_specs=[
            pl.BlockSpec((block_rows, width), lambda i: (i, 0)),
            pl.BlockSpec((block_count, lanes), lambda i: (0, 0)),
        ],
        compiler_params=pltpu.CompilerParams(
            dimension_semantics=("arbitrary",), vmem_limit_bytes=VMEM_LIMIT
        ),
        cost_estimate=SMALL,
        name="adagrad",
    )(grads, accum, table)


def pack_bags(blocks, entries, weights, targets):
    per_tile, _, owner_count = blocks.shape
    lanes = entries.shape[1] // owner_count
    entry_count = entries.shape[0]
    span = per_tile * lanes // entry_count
    group = owner_count // 2

    def kernel(blocks_ref, entries_ref, weights_ref, targets_ref, out_ref):
        shift = lax.broadcasted_iota(jnp.int32, (entry_count, lanes), 0) * span
        lane = lax.broadcasted_iota(jnp.int32, (1, lanes), 1)

        def bags(e, carry):
            for u in range(4):
                i = 4 * e + u
                d = pl.program_id(0) * group + i
                at = pl.ds(pl.multiple_of(i * lanes, lanes), lanes)
                chosen = jnp.zeros((1, lanes), jnp.int32)
                for b in range(per_tile):
                    chosen = jnp.where(lane == b, blocks_ref[b, 0, d], chosen)
                bag = jnp.concatenate(
                    [
                        (entries_ref[:, at] - shift).astype(jnp.float32),
                        weights_ref[:, at],
                        (targets_ref[:, at] - 256).astype(jnp.float32),
                        chosen.astype(jnp.float32),
                        jnp.zeros((TILE - 2 * entry_count - 2, lanes), jnp.float32),
                    ],
                    axis=0,
                )
                out_ref[i] = bag.astype(out_ref.dtype)
            return carry

        lax.fori_loop(0, group // 4, bags, 0)

    return pl.pallas_call(
        kernel,
        out_shape=jax.ShapeDtypeStruct((owner_count, TILE, lanes), jnp.bfloat16),
        grid=(owner_count // group,),
        in_specs=[
            pl.BlockSpec(memory_space=pltpu.SMEM),
            pl.BlockSpec((entry_count, group * lanes), lambda i: (0, i)),
            pl.BlockSpec((entry_count, group * lanes), lambda i: (0, i)),
            pl.BlockSpec((1, group * lanes), lambda i: (0, i)),
        ],
        out_specs=pl.BlockSpec((group, TILE, lanes), lambda i: (i, 0, 0)),
        compiler_params=pltpu.CompilerParams(
            dimension_semantics=("arbitrary",), vmem_limit_bytes=ALL_VMEM
        ),
        cost_estimate=SMALL,
        name="pack_bags",
    )(blocks, entries, weights, targets)


def pack_parts(grads):
    count, rows, width = grads.shape
    lanes = 128
    sides = width // lanes
    receivers = rows // TILE * sides

    def kernel(grads_ref, out_ref):
        def cut(i, carry):
            for g in range(rows // TILE):
                for h in range(sides):
                    out_ref[g * sides + h, i] = grads_ref[i, pl.ds(g * TILE, TILE), pl.ds(h * lanes, lanes)]
            return carry

        lax.fori_loop(0, TAIL, cut, 0)

    return pl.pallas_call(
        kernel,
        out_shape=jax.ShapeDtypeStruct((receivers, count + TAIL, TILE, lanes), grads.dtype),
        grid=(count // TAIL,),
        in_specs=[pl.BlockSpec((TAIL, rows, width), lambda i: (i, 0, 0))],
        out_specs=pl.BlockSpec((receivers, TAIL, TILE, lanes), lambda i: (0, i, 0, 0)),
        compiler_params=pltpu.CompilerParams(
            dimension_semantics=("arbitrary",), vmem_limit_bytes=VMEM_LIMIT
        ),
        cost_estimate=SMALL,
        name="pack_parts",
    )(grads)


def add_bags(place, packed, owners, numbers, bags, parts, block_count):
    receivers, tiles, _, lanes = packed.shape
    count = owners.shape[1]
    kept = TAIL - 1

    def kernel(place_ref, packed_ref, owners_ref, numbers_ref, bags_ref, out_ref, row_ref):
        row_ref[...] = jnp.zeros_like(row_ref)
        row_ref[0:1, 0:count] = (owners_ref[...] * block_count + numbers_ref[...]).astype(jnp.float32)
        slots = row_ref[...].astype(out_ref.dtype)
        for t in range(receivers):
            u, j = t // parts, t % parts
            group = (j + parts - place_ref[1] - u) % parts
            out_ref[t, 0] = slots
            for b in range(kept):
                out_ref[t, 1 + b] = bags_ref[(2 * b + group % 2) * kept + group // 2, u]

    whole = pl.BlockSpec(memory_space=pltpu.VMEM)
    return pl.pallas_call(
        kernel,
        out_shape=jax.ShapeDtypeStruct(packed.shape, packed.dtype),
        grid=(1,),
        in_specs=[pl.BlockSpec(memory_space=pltpu.SMEM), pl.BlockSpec(memory_space=pl.ANY), whole, whole, whole],
        out_specs=pl.BlockSpec((receivers, TAIL, TILE, lanes), lambda i: (0, tiles // TAIL - 1, 0, 0)),
        scratch_shapes=[pltpu.VMEM((TILE, lanes), jnp.float32)],
        input_output_aliases={1: 0},
        compiler_params=pltpu.CompilerParams(vmem_limit_bytes=VMEM_LIMIT),
        cost_estimate=SMALL,
        name="add_bags",
    )(place, packed, owners, numbers, bags)


def add_parts(arrived, count, parts, slot_count, highs):
    sources, _, _, lanes = arrived.shape
    kept = TAIL - 1
    lows = sources // parts
    each = slot_count // highs

    def kernel(recv_ref, out_ref, bags_ref, acc_ref, numbers_ref, slots_ref, sem):
        for t in range(sources):
            numbers_ref[pl.ds(t, 1), :] = recv_ref[t, count].astype(jnp.float32)[0:1].astype(jnp.int32)
        copy = pltpu.make_async_copy(numbers_ref, slots_ref, sem)
        copy.start()
        acc_ref[...] = jnp.zeros_like(acc_ref)
        for t in range(sources):
            for b in range(kept):
                bags_ref[t % parts, b * lows + t // parts] = recv_ref[t, count + 1 + b]
        copy.wait()

        def add(i, carry):
            for t in range(sources):
                slot = slots_ref[t, i]
                acc_ref[slot] = acc_ref[slot] + recv_ref[t, i].astype(jnp.float32)
            return carry

        lax.fori_loop(0, count, add, 0)

        def place(e, carry):
            for i in range(each):
                out_ref[e, pl.ds(i * TILE, TILE), :] = acc_ref[e * each + i].astype(out_ref.dtype)
            return carry

        lax.fori_loop(0, highs, place, 0)

    whole = pl.BlockSpec(memory_space=pltpu.VMEM)
    return pl.pallas_call(
        kernel,
        out_shape=[
            jax.ShapeDtypeStruct((highs, each * TILE, lanes), jnp.bfloat16),
            jax.ShapeDtypeStruct((parts, lows * kept, TILE, lanes), jnp.bfloat16),
        ],
        in_specs=[whole],
        out_specs=[whole] * 2,
        scratch_shapes=[
            pltpu.VMEM((slot_count, TILE, lanes), jnp.float32),
            pltpu.VMEM((sources, lanes), jnp.int32),
            pltpu.SMEM((sources, lanes), jnp.int32),
            pltpu.SemaphoreType.DMA(()),
        ],
        compiler_params=pltpu.CompilerParams(vmem_limit_bytes=VMEM_LIMIT),
        cost_estimate=SMALL,
        name="add_parts",
    )(arrived)


def add_sources(received, lows, parts):
    sources, rows, lanes = received.shape
    each = rows // lows
    tile = 32

    def kernel(recv_ref, out_ref):
        for u in range(lows):
            for first in range(0, each, tile):
                at = pl.ds(u * each + first, tile)
                total = recv_ref[0, at, :].astype(jnp.float32)
                for e in range(1, sources):
                    total = total + recv_ref[e, at, :].astype(jnp.float32)
                total = total.astype(out_ref.dtype)
                for r in range(parts):
                    out_ref[u * parts + r, pl.ds(first, tile), :] = total

    whole = pl.BlockSpec(memory_space=pltpu.VMEM)
    return pl.pallas_call(
        kernel,
        out_shape=jax.ShapeDtypeStruct((lows * parts, each, lanes), jnp.bfloat16),
        in_specs=[whole],
        out_specs=whole,
        compiler_params=pltpu.CompilerParams(vmem_limit_bytes=VMEM_LIMIT),
        cost_estimate=SMALL,
        name="add_sources",
    )(received)


def pool_parts(first, kind, place, table, bags):
    owner_count, block_count, width, lanes = table.shape
    parts = bags.shape[0]
    many = parts // 2
    per_tile = 3
    entry_count = 4
    span = per_tile * lanes // entry_count
    samples = SAMPLES

    def kernel(place_ref, table_ref, bags_ref, out_ref, numbers_ref, blocks_ref, sem):
        step = pl.program_id(0)
        replica = place_ref[0] ^ (2 * step + first)

        @pl.when(step == 0)
        def _():
            for i in range(many):
                r = place_ref[0] ^ (2 * i + first)
                for p in range(owner_count):
                    numbers_ref[pl.ds(i * owner_count + p, 1), :] = (
                        bags_ref[r, p].astype(jnp.float32)[2 * entry_count + 1 : 2 * entry_count + 2].astype(jnp.int32)
                    )
            copy = pltpu.make_async_copy(numbers_ref, blocks_ref, sem)
            copy.start()
            copy.wait()

        position = lax.broadcasted_iota(jnp.int32, (span, lanes), 0)
        sample = lax.broadcasted_iota(jnp.int32, (samples, owner_count * lanes), 0)
        partials, targets = [], []
        for p in range(owner_count):
            bag = bags_ref[replica, p].astype(jnp.float32)
            entries = bag[0:entry_count].astype(jnp.int32)
            weights = bag[entry_count : 2 * entry_count]
            targets.append(bag[2 * entry_count : 2 * entry_count + 1].astype(jnp.int32) + 256)
            incidence = jnp.concatenate(
                [
                    jnp.where(position == entries[l : l + 1], weights[l : l + 1], 0.0)
                    for l in range(entry_count)
                ],
                axis=0,
            ).astype(jnp.bfloat16)
            chosen = [blocks_ref[step * owner_count + p, j] for j in range(per_tile)]
            slab = jnp.concatenate([table_ref[p, b] for b in chosen], axis=1)
            partials.append(
                jnp.dot(slab, incidence, preferred_element_type=jnp.float32).astype(jnp.bfloat16)
            )
        selector = jnp.where(sample == jnp.concatenate(targets, axis=1), 1.0, 0.0).astype(jnp.bfloat16)
        out_ref[0] = lax.dot_general(
            selector,
            jnp.concatenate(partials, axis=1),
            (((1,), (1,)), ((), ())),
            preferred_element_type=jnp.float32,
        ).astype(kind)

    whole = pl.BlockSpec(memory_space=pltpu.VMEM)
    return pl.pallas_call(
        kernel,
        out_shape=jax.ShapeDtypeStruct((many, samples, width), kind),
        grid=(many,),
        in_specs=[pl.BlockSpec(memory_space=pltpu.SMEM), whole, whole],
        out_specs=pl.BlockSpec((1, samples, width), lambda i: (i, 0, 0)),
        scratch_shapes=[
            pltpu.VMEM((many * owner_count, lanes), jnp.int32),
            pltpu.SMEM((many * owner_count, lanes), jnp.int32),
            pltpu.SemaphoreType.DMA(()),
        ],
        compiler_params=pltpu.CompilerParams(
            dimension_semantics=("arbitrary",), vmem_limit_bytes=VMEM_LIMIT
        ),
        cost_estimate=SMALL,
        name="pool_parts",
    )(place, table, bags)


def join(mine, theirs):
    many, samples, width = mine.shape
    tile = samples // 4

    def kernel(mine_ref, theirs_ref, *out_refs):
        for i in range(many):
            out_refs[i][...] = (mine_ref[i] + theirs_ref[i].astype(jnp.float32)).astype(jnp.bfloat16)

    block = pl.BlockSpec((many, tile, width), lambda i: (0, i, 0))
    return pl.pallas_call(
        kernel,
        out_shape=[jax.ShapeDtypeStruct((samples, width), jnp.bfloat16)] * many,
        grid=(samples // tile,),
        in_specs=[block] * 2,
        out_specs=[pl.BlockSpec((tile, width), lambda i: (i, 0))] * many,
        compiler_params=pltpu.CompilerParams(
            dimension_semantics=("arbitrary",), vmem_limit_bytes=VMEM_LIMIT
        ),
        cost_estimate=SMALL,
        name="join",
    )(mine, theirs)


def cross_layers(pooled_parts, other_feats, cross_w, cross_b):
    parts = len(pooled_parts)
    samples, width = pooled_parts[0].shape
    layers, full, _ = cross_w.shape
    tile = 128

    def kernel(*refs):
        feats_ref, w_ref, b_ref, out_ref = refs[parts:]
        pooled = refs[0][...].astype(jnp.float32)
        for j in range(1, parts):
            pooled = pooled + refs[j][...].astype(jnp.float32)
        first = jnp.concatenate([pooled, feats_ref[...].astype(jnp.float32)], axis=1)
        crossed = first
        for layer in range(layers):
            mixing = (
                jnp.dot(crossed.astype(jnp.bfloat16), w_ref[layer], preferred_element_type=jnp.float32)
                + b_ref[layer : layer + 1, :]
            )
            crossed = first * mixing + crossed
        out_ref[...] = crossed.astype(out_ref.dtype)

    return pl.pallas_call(
        kernel,
        out_shape=jax.ShapeDtypeStruct((samples, full), jnp.bfloat16),
        grid=(samples // tile,),
        in_specs=[
            *[pl.BlockSpec((tile, width), lambda i: (i, 0))] * parts,
            pl.BlockSpec((tile, full - width), lambda i: (i, 0)),
            pl.BlockSpec((layers, full, full), lambda i: (0, 0, 0)),
            pl.BlockSpec((layers, full), lambda i: (0, 0)),
        ],
        out_specs=pl.BlockSpec((tile, full), lambda i: (i, 0)),
        compiler_params=pltpu.CompilerParams(
            dimension_semantics=("arbitrary",), vmem_limit_bytes=VMEM_LIMIT
        ),
        cost_estimate=SMALL,
        name="cross_layers",
    )(*pooled_parts, other_feats, cross_w, cross_b)


def local(
    table,
    accum,
    bag_blocks,
    bag_entries,
    bag_weights,
    bag_target,
    other_feats,
    cross_w,
    cross_b,
    evict_grads,
    evict_owner,
    evict_block,
):
    parts = lax.axis_size("replica")
    count, block_rows, width = evict_grads.shape[1:]
    slab_rows = table.shape[0]
    block_count = slab_rows // block_rows
    highs = lax.axis_size(HIGHS)
    lows = lax.axis_size("yl")
    me = lax.axis_index("replica").astype(jnp.int32)
    y = lax.axis_index(("yh", "yl")).astype(jnp.int32)
    place = jnp.stack([me, y - y % lows])

    def to_replica(array, k):
        return lax.ppermute(array, "replica", [(r, r ^ k) for r in range(parts)])

    with jax.named_scope("table_gather"):
        slab = lax.optimization_barrier(table).astype(jnp.bfloat16)
        slab = slab.reshape(block_count, block_rows, width).transpose(0, 2, 1)
        moves = []
        for owner in range(SIDE * SIDE):
            z, y_own = owner // SIDE, owner % SIDE
            to_z, group = z // 2 * 2 + y_own % 2, y_own // 2 * 2 + z % 2
            moves += [(owner * parts + r, (to_z * SIDE + (r - group) % SIDE) * parts + r) for r in range(parts)]
        moved = lax.ppermute(slab, (*MP, "replica"), moves)
        slabs = lax.all_gather(moved, "z", axis=0)

    with jax.named_scope("bags_over_high"):
        bags = pack_bags(bag_blocks.transpose(2, 0, 1), bag_entries[0].T, bag_weights[0].T, bag_target)
        bags = bags.reshape(highs, lows, TILE, bags.shape[2])
        bags = lax.all_to_all(bags, HIGHS, split_axis=0, concat_axis=0, tiled=True)
        bags, _ = lax.optimization_barrier((bags, moved))

    with jax.named_scope("parts_over_low"):
        packed = pack_parts(evict_grads[0])
        sent = add_bags(place, packed, evict_owner[:, :, 0], evict_block, bags, parts, block_count)
        arrived = lax.all_to_all(sent, LOWS, split_axis=0, concat_axis=0, tiled=True)

    with jax.named_scope("sums_over_high"):
        sums, bags = add_parts(arrived, count, parts, highs * lows * block_count, highs)
        received = lax.all_to_all(sums, HIGHS, split_axis=0, concat_axis=0, tiled=True)

    with jax.named_scope("pooling"):
        others = pool_parts(1, jnp.bfloat16, place, slabs, bags)
        mine = pool_parts(0, jnp.float32, place, slabs, bags)
        joined = join(mine, to_replica(others, 1))
        pooled = [joined[0]] + [to_replica(joined[i], 2 * i) for i in (2, 3, 1)]

    with jax.named_scope("sums_to_owners"):
        received, _ = lax.optimization_barrier((received, pooled))
        shared = add_sources(received, lows, parts)
        grads = lax.all_to_all(shared, LOWS, split_axis=0, concat_axis=0, tiled=True)

    with jax.named_scope("table_update"):
        new_table, new_accum = adagrad(grads, accum.reshape(block_count, block_rows), table)
        new_accum = new_accum.reshape(slab_rows)

    with jax.named_scope("cross"):
        cross_out = cross_layers(pooled, other_feats[0], cross_w, cross_b)
    return (cross_out[None], new_table, new_accum)


def solution(mesh):
    parts = mesh.shape["replica"]
    fine = Mesh(mesh.devices.reshape(SIDE, SIDE // 2, 2, parts), (*MP, "replica"))
    in_specs = (
        P(MP, None),
        P(MP),
        P("replica", MP, None),
        P("replica", MP, None),
        P("replica", MP, None),
        P("replica", MP),
        P("replica", MP, None),
        P(),
        P(),
        P("replica", MP, None, None),
        P("replica", MP, None),
        P("replica", MP),
    )
    out_specs = (P("replica", MP, None), P(MP, None), P(MP))
    return jax.shard_map(local, mesh=fine, in_specs=in_specs, out_specs=out_specs, check_vma=False)
```

```python
import jax
import jax.numpy as jnp
from jax import lax
from jax.experimental import pallas as pl
from jax.experimental.pallas import tpu as pltpu
from jax.sharding import Mesh
from jax.sharding import PartitionSpec as P

VMEM_LIMIT = 48 * 1024 * 1024
ALL_VMEM = 60 * 1024 * 1024
learn_rate = 0.3
TILE = 16
SMALL = pl.CostEstimate(flops=1000, bytes_accessed=1000, transcendentals=0)
TAIL = 5
SAMPLES = 512
LOWS = ("yl", "replica")
HIGHS = ("z", "yh")
MP = ("z", "yh", "yl")
SIDE = 8


def adagrad(grads, accum, table):
    sources, rows, lanes = grads.shape
    slab_rows, width = table.shape
    sides = width // lanes
    block_count = rows // TILE
    block_rows = slab_rows // block_count

    def kernel(grads_ref, accum_ref, table_ref, new_table_ref, new_accum_ref):
        block = pl.program_id(0)
        gradient = jnp.concatenate(
            [
                jnp.concatenate([grads_ref[t + h].astype(jnp.float32) for h in range(sides)], axis=1)
                for t in range(0, sources, sides)
            ],
            axis=0,
        )
        mean = jnp.sum(gradient * gradient, axis=1, keepdims=True) * (1.0 / width)
        old = jnp.broadcast_to(accum_ref[pl.ds(block, 1), :], (block_rows, lanes)).T
        fresh = old + mean
        new_accum_ref[pl.ds(block, 1), :] = fresh.T[0:1]
        root = jnp.sqrt(fresh)
        for h in range(sides):
            at = slice(h * lanes, (h + 1) * lanes)
            new_table_ref[:, at] = table_ref[:, at] - learn_rate * gradient[:, at] / root

    return pl.pallas_call(
        kernel,
        out_shape=[
            jax.ShapeDtypeStruct((slab_rows, width), jnp.float32),
            jax.ShapeDtypeStruct((block_count, lanes), jnp.float32),
        ],
        grid=(block_count,),
        in_specs=[
            pl.BlockSpec((sources, TILE, lanes), lambda i: (0, i, 0)),
            pl.BlockSpec((block_count, lanes), lambda i: (0, 0)),
            pl.BlockSpec((block_rows, width), lambda i: (i, 0)),
        ],
        out_specs=[
            pl.BlockSpec((block_rows, width), lambda i: (i, 0)),
            pl.BlockSpec((block_count, lanes), lambda i: (0, 0)),
        ],
        compiler_params=pltpu.CompilerParams(
            dimension_semantics=("arbitrary",), vmem_limit_bytes=VMEM_LIMIT
        ),
        cost_estimate=SMALL,
        name="adagrad",
    )(grads, accum, table)


def pack_bags(blocks, entries, weights, targets):
    per_tile, _, owner_count = blocks.shape
    lanes = entries.shape[1] // owner_count
    entry_count = entries.shape[0]
    span = per_tile * lanes // entry_count
    group = owner_count // 2

    def kernel(blocks_ref, entries_ref, weights_ref, targets_ref, out_ref):
        shift = lax.broadcasted_iota(jnp.int32, (entry_count, lanes), 0) * span
        lane = lax.broadcasted_iota(jnp.int32, (1, lanes), 1)

        def bags(e, carry):
            for u in range(4):
                i = 4 * e + u
                d = pl.program_id(0) * group + i
                at = pl.ds(pl.multiple_of(i * lanes, lanes), lanes)
                chosen = jnp.zeros((1, lanes), jnp.int32)
                for b in range(per_tile):
                    chosen = jnp.where(lane == b, blocks_ref[b, 0, d], chosen)
                bag = jnp.concatenate(
                    [
                        (entries_ref[:, at] - shift).astype(jnp.float32),
                        weights_ref[:, at],
                        (targets_ref[:, at] - 256).astype(jnp.float32),
                        chosen.astype(jnp.float32),
                        jnp.zeros((TILE - 2 * entry_count - 2, lanes), jnp.float32),
                    ],
                    axis=0,
                )
                out_ref[i] = bag.astype(out_ref.dtype)
            return carry

        lax.fori_loop(0, group // 4, bags, 0)

    return pl.pallas_call(
        kernel,
        out_shape=jax.ShapeDtypeStruct((owner_count, TILE, lanes), jnp.bfloat16),
        grid=(owner_count // group,),
        in_specs=[
            pl.BlockSpec(memory_space=pltpu.SMEM),
            pl.BlockSpec((entry_count, group * lanes), lambda i: (0, i)),
            pl.BlockSpec((entry_count, group * lanes), lambda i: (0, i)),
            pl.BlockSpec((1, group * lanes), lambda i: (0, i)),
        ],
        out_specs=pl.BlockSpec((group, TILE, lanes), lambda i: (i, 0, 0)),
        compiler_params=pltpu.CompilerParams(
            dimension_semantics=("arbitrary",), vmem_limit_bytes=ALL_VMEM
        ),
        cost_estimate=SMALL,
        name="pack_bags",
    )(blocks, entries, weights, targets)


def pack_parts(grads):
    count, rows, width = grads.shape
    lanes = 128
    sides = width // lanes
    receivers = rows // TILE * sides

    def kernel(grads_ref, out_ref):
        def cut(i, carry):
            for g in range(rows // TILE):
                for h in range(sides):
                    out_ref[g * sides + h, i] = grads_ref[i, pl.ds(g * TILE, TILE), pl.ds(h * lanes, lanes)]
            return carry

        lax.fori_loop(0, TAIL, cut, 0)

    return pl.pallas_call(
        kernel,
        out_shape=jax.ShapeDtypeStruct((receivers, count + TAIL, TILE, lanes), grads.dtype),
        grid=(count // TAIL,),
        in_specs=[pl.BlockSpec((TAIL, rows, width), lambda i: (i, 0, 0))],
        out_specs=pl.BlockSpec((receivers, TAIL, TILE, lanes), lambda i: (0, i, 0, 0)),
        compiler_params=pltpu.CompilerParams(
            dimension_semantics=("arbitrary",), vmem_limit_bytes=VMEM_LIMIT
        ),
        cost_estimate=SMALL,
        name="pack_parts",
    )(grads)


def add_bags(place, packed, owners, numbers, bags, parts, block_count):
    receivers, tiles, _, lanes = packed.shape
    count = owners.shape[1]
    kept = TAIL - 1

    def kernel(place_ref, packed_ref, owners_ref, numbers_ref, bags_ref, out_ref, row_ref):
        row_ref[...] = jnp.zeros_like(row_ref)
        row_ref[0:1, 0:count] = (owners_ref[...] * block_count + numbers_ref[...]).astype(jnp.float32)
        slots = row_ref[...].astype(out_ref.dtype)
        for t in range(receivers):
            u, j = t // parts, t % parts
            group = (j + parts - place_ref[1] - u) % parts
            out_ref[t, 0] = slots
            for b in range(kept):
                out_ref[t, 1 + b] = bags_ref[(2 * b + group % 2) * kept + group // 2, u]

    whole = pl.BlockSpec(memory_space=pltpu.VMEM)
    return pl.pallas_call(
        kernel,
        out_shape=jax.ShapeDtypeStruct(packed.shape, packed.dtype),
        grid=(1,),
        in_specs=[pl.BlockSpec(memory_space=pltpu.SMEM), pl.BlockSpec(memory_space=pl.ANY), whole, whole, whole],
        out_specs=pl.BlockSpec((receivers, TAIL, TILE, lanes), lambda i: (0, tiles // TAIL - 1, 0, 0)),
        scratch_shapes=[pltpu.VMEM((TILE, lanes), jnp.float32)],
        input_output_aliases={1: 0},
        compiler_params=pltpu.CompilerParams(vmem_limit_bytes=VMEM_LIMIT),
        cost_estimate=SMALL,
        name="add_bags",
    )(place, packed, owners, numbers, bags)


def add_parts(arrived, count, parts, slot_count, highs):
    sources, _, _, lanes = arrived.shape
    kept = TAIL - 1
    lows = sources // parts
    each = slot_count // highs
    chunks = 4
    chunk = highs // chunks

    def kernel(recv_ref, out_ref, bags_ref, acc_ref, stage_ref, numbers_ref, slots_ref, sem, out_sems):
        for t in range(sources):
            numbers_ref[pl.ds(t, 1), :] = recv_ref[t, count].astype(jnp.float32)[0:1].astype(jnp.int32)
        copy = pltpu.make_async_copy(numbers_ref, slots_ref, sem)
        copy.start()
        acc_ref[...] = jnp.zeros_like(acc_ref)
        for t in range(sources):
            for b in range(kept):
                bags_ref[t % parts, b * lows + t // parts] = recv_ref[t, count + 1 + b]
        copy.wait()

        def add(i, carry):
            for t in range(sources):
                slot = slots_ref[t, i]
                acc_ref[slot] = acc_ref[slot] + recv_ref[t, i].astype(jnp.float32)
            return carry

        lax.fori_loop(0, count, add, 0)

        def place(e, carry):
            for i in range(each):
                stage_ref[e, pl.ds(i * TILE, TILE), :] = acc_ref[e * each + i].astype(stage_ref.dtype)
            return carry

        copies = []
        for n in range(chunks):
            lax.fori_loop(n * chunk, (n + 1) * chunk, place, 0)
            at = pl.ds(n * chunk, chunk)
            copies.append(pltpu.make_async_copy(stage_ref.at[at], out_ref.at[at], out_sems.at[n]))
            copies[-1].start()
        for out_copy in copies:
            out_copy.wait()

    whole = pl.BlockSpec(memory_space=pltpu.VMEM)
    return pl.pallas_call(
        kernel,
        out_shape=[
            jax.ShapeDtypeStruct((highs, each * TILE, lanes), jnp.bfloat16),
            jax.ShapeDtypeStruct((parts, lows * kept, TILE, lanes), jnp.bfloat16),
        ],
        in_specs=[whole],
        out_specs=[pl.BlockSpec(memory_space=pltpu.HBM), whole],
        scratch_shapes=[
            pltpu.VMEM((slot_count, TILE, lanes), jnp.float32),
            pltpu.VMEM((highs, each * TILE, lanes), jnp.bfloat16),
            pltpu.VMEM((sources, lanes), jnp.int32),
            pltpu.SMEM((sources, lanes), jnp.int32),
            pltpu.SemaphoreType.DMA(()),
            pltpu.SemaphoreType.DMA((chunks,)),
        ],
        compiler_params=pltpu.CompilerParams(vmem_limit_bytes=VMEM_LIMIT),
        cost_estimate=SMALL,
        name="add_parts",
    )(arrived)


def add_sources(received, lows, parts):
    sources, rows, lanes = received.shape
    each = rows // lows
    tile = 32

    def kernel(recv_ref, out_ref):
        for u in range(lows):
            for first in range(0, each, tile):
                at = pl.ds(u * each + first, tile)
                total = recv_ref[0, at, :].astype(jnp.float32)
                for e in range(1, sources):
                    total = total + recv_ref[e, at, :].astype(jnp.float32)
                total = total.astype(out_ref.dtype)
                for r in range(parts):
                    out_ref[u * parts + r, pl.ds(first, tile), :] = total

    whole = pl.BlockSpec(memory_space=pltpu.VMEM)
    return pl.pallas_call(
        kernel,
        out_shape=jax.ShapeDtypeStruct((lows * parts, each, lanes), jnp.bfloat16),
        in_specs=[whole],
        out_specs=whole,
        compiler_params=pltpu.CompilerParams(vmem_limit_bytes=VMEM_LIMIT),
        cost_estimate=SMALL,
        name="add_sources",
    )(received)


def pool_parts(first, kind, place, table, bags):
    owner_count, block_count, width, lanes = table.shape
    parts = bags.shape[0]
    many = parts // 2
    per_tile = 3
    entry_count = 4
    span = per_tile * lanes // entry_count
    samples = SAMPLES

    def kernel(place_ref, table_ref, bags_ref, out_ref, numbers_ref, blocks_ref, sem):
        step = pl.program_id(0)
        replica = place_ref[0] ^ (2 * step + first)

        @pl.when(step == 0)
        def _():
            for i in range(many):
                r = place_ref[0] ^ (2 * i + first)
                for p in range(owner_count):
                    numbers_ref[pl.ds(i * owner_count + p, 1), :] = (
                        bags_ref[r, p].astype(jnp.float32)[2 * entry_count + 1 : 2 * entry_count + 2].astype(jnp.int32)
                    )
            copy = pltpu.make_async_copy(numbers_ref, blocks_ref, sem)
            copy.start()
            copy.wait()

        position = lax.broadcasted_iota(jnp.int32, (span, lanes), 0)
        sample = lax.broadcasted_iota(jnp.int32, (samples, owner_count * lanes), 0)
        partials, targets = [], []
        for p in range(owner_count):
            bag = bags_ref[replica, p].astype(jnp.float32)
            entries = bag[0:entry_count].astype(jnp.int32)
            weights = bag[entry_count : 2 * entry_count]
            targets.append(bag[2 * entry_count : 2 * entry_count + 1].astype(jnp.int32) + 256)
            incidence = jnp.concatenate(
                [
                    jnp.where(position == entries[l : l + 1], weights[l : l + 1], 0.0)
                    for l in range(entry_count)
                ],
                axis=0,
            ).astype(jnp.bfloat16)
            chosen = [blocks_ref[step * owner_count + p, j] for j in range(per_tile)]
            slab = jnp.concatenate([table_ref[p, b] for b in chosen], axis=1)
            partials.append(
                jnp.dot(slab, incidence, preferred_element_type=jnp.float32).astype(jnp.bfloat16)
            )
        selector = jnp.where(sample == jnp.concatenate(targets, axis=1), 1.0, 0.0).astype(jnp.bfloat16)
        out_ref[0] = lax.dot_general(
            selector,
            jnp.concatenate(partials, axis=1),
            (((1,), (1,)), ((), ())),
            preferred_element_type=jnp.float32,
        ).astype(kind)

    whole = pl.BlockSpec(memory_space=pltpu.VMEM)
    return pl.pallas_call(
        kernel,
        out_shape=jax.ShapeDtypeStruct((many, samples, width), kind),
        grid=(many,),
        in_specs=[pl.BlockSpec(memory_space=pltpu.SMEM), whole, whole],
        out_specs=pl.BlockSpec((1, samples, width), lambda i: (i, 0, 0)),
        scratch_shapes=[
            pltpu.VMEM((many * owner_count, lanes), jnp.int32),
            pltpu.SMEM((many * owner_count, lanes), jnp.int32),
            pltpu.SemaphoreType.DMA(()),
        ],
        compiler_params=pltpu.CompilerParams(
            dimension_semantics=("arbitrary",), vmem_limit_bytes=VMEM_LIMIT
        ),
        cost_estimate=SMALL,
        name="pool_parts",
    )(place, table, bags)


def join(mine, theirs):
    many, samples, width = mine.shape
    tile = samples // 4

    def kernel(mine_ref, theirs_ref, *out_refs):
        for i in range(many):
            out_refs[i][...] = (mine_ref[i] + theirs_ref[i].astype(jnp.float32)).astype(jnp.bfloat16)

    block = pl.BlockSpec((many, tile, width), lambda i: (0, i, 0))
    return pl.pallas_call(
        kernel,
        out_shape=[jax.ShapeDtypeStruct((samples, width), jnp.bfloat16)] * many,
        grid=(samples // tile,),
        in_specs=[block] * 2,
        out_specs=[pl.BlockSpec((tile, width), lambda i: (i, 0))] * many,
        compiler_params=pltpu.CompilerParams(
            dimension_semantics=("arbitrary",), vmem_limit_bytes=VMEM_LIMIT
        ),
        cost_estimate=SMALL,
        name="join",
    )(mine, theirs)


def cross_layers(pooled_parts, other_feats, cross_w, cross_b):
    parts = len(pooled_parts)
    samples, width = pooled_parts[0].shape
    layers, full, _ = cross_w.shape
    tile = 128

    def kernel(*refs):
        feats_ref, w_ref, b_ref, out_ref = refs[parts:]
        pooled = refs[0][...].astype(jnp.float32)
        for j in range(1, parts):
            pooled = pooled + refs[j][...].astype(jnp.float32)
        first = jnp.concatenate([pooled, feats_ref[...].astype(jnp.float32)], axis=1)
        crossed = first
        for layer in range(layers):
            mixing = (
                jnp.dot(crossed.astype(jnp.bfloat16), w_ref[layer], preferred_element_type=jnp.float32)
                + b_ref[layer : layer + 1, :]
            )
            crossed = first * mixing + crossed
        out_ref[...] = crossed.astype(out_ref.dtype)

    return pl.pallas_call(
        kernel,
        out_shape=jax.ShapeDtypeStruct((samples, full), jnp.bfloat16),
        grid=(samples // tile,),
        in_specs=[
            *[pl.BlockSpec((tile, width), lambda i: (i, 0))] * parts,
            pl.BlockSpec((tile, full - width), lambda i: (i, 0)),
            pl.BlockSpec((layers, full, full), lambda i: (0, 0, 0)),
            pl.BlockSpec((layers, full), lambda i: (0, 0)),
        ],
        out_specs=pl.BlockSpec((tile, full), lambda i: (i, 0)),
        compiler_params=pltpu.CompilerParams(
            dimension_semantics=("arbitrary",), vmem_limit_bytes=VMEM_LIMIT
        ),
        cost_estimate=SMALL,
        name="cross_layers",
    )(*pooled_parts, other_feats, cross_w, cross_b)


def local(
    table,
    accum,
    bag_blocks,
    bag_entries,
    bag_weights,
    bag_target,
    other_feats,
    cross_w,
    cross_b,
    evict_grads,
    evict_owner,
    evict_block,
):
    parts = lax.axis_size("replica")
    count, block_rows, width = evict_grads.shape[1:]
    slab_rows = table.shape[0]
    block_count = slab_rows // block_rows
    highs = lax.axis_size(HIGHS)
    lows = lax.axis_size("yl")
    me = lax.axis_index("replica").astype(jnp.int32)
    y = lax.axis_index(("yh", "yl")).astype(jnp.int32)
    place = jnp.stack([me, y - y % lows])

    def to_replica(array, k):
        return lax.ppermute(array, "replica", [(r, r ^ k) for r in range(parts)])

    with jax.named_scope("table_gather"):
        slab = lax.optimization_barrier(table).astype(jnp.bfloat16)
        slab = slab.reshape(block_count, block_rows, width).transpose(0, 2, 1)
        moves = []
        for owner in range(SIDE * SIDE):
            z, y_own = owner // SIDE, owner % SIDE
            to_z, group = z // 2 * 2 + y_own % 2, y_own // 2 * 2 + z % 2
            moves += [(owner * parts + r, (to_z * SIDE + (r - group) % SIDE) * parts + r) for r in range(parts)]
        moved = lax.ppermute(slab, (*MP, "replica"), moves)
        slabs = lax.all_gather(moved, "z", axis=0)

    with jax.named_scope("bags_over_high"):
        bags = pack_bags(bag_blocks.transpose(2, 0, 1), bag_entries[0].T, bag_weights[0].T, bag_target)
        bags = bags.reshape(highs, lows, TILE, bags.shape[2])
        bags = lax.all_to_all(bags, HIGHS, split_axis=0, concat_axis=0, tiled=True)
        bags, _ = lax.optimization_barrier((bags, moved))

    with jax.named_scope("parts_over_low"):
        packed = pack_parts(evict_grads[0])
        sent = add_bags(place, packed, evict_owner[:, :, 0], evict_block, bags, parts, block_count)
        arrived = lax.all_to_all(sent, LOWS, split_axis=0, concat_axis=0, tiled=True)

    with jax.named_scope("sums_over_high"):
        sums, bags = add_parts(arrived, count, parts, highs * lows * block_count, highs)
        received = lax.all_to_all(sums, HIGHS, split_axis=0, concat_axis=0, tiled=True)

    with jax.named_scope("pooling"):
        others = pool_parts(1, jnp.bfloat16, place, slabs, bags)
        mine = pool_parts(0, jnp.float32, place, slabs, bags)
        joined = join(mine, to_replica(others, 1))
        pooled = [joined[0]] + [to_replica(joined[i], 2 * i) for i in (2, 3, 1)]

    with jax.named_scope("sums_to_owners"):
        received, _ = lax.optimization_barrier((received, pooled))
        shared = add_sources(received, lows, parts)
        grads = lax.all_to_all(shared, LOWS, split_axis=0, concat_axis=0, tiled=True)

    with jax.named_scope("table_update"):
        new_table, new_accum = adagrad(grads, accum.reshape(block_count, block_rows), table)
        new_accum = new_accum.reshape(slab_rows)

    with jax.named_scope("cross"):
        cross_out = cross_layers(pooled, other_feats[0], cross_w, cross_b)
    return (cross_out[None], new_table, new_accum)


def solution(mesh):
    parts = mesh.shape["replica"]
    fine = Mesh(mesh.devices.reshape(SIDE, SIDE // 2, 2, parts), (*MP, "replica"))
    in_specs = (
        P(MP, None),
        P(MP),
        P("replica", MP, None),
        P("replica", MP, None),
        P("replica", MP, None),
        P("replica", MP),
        P("replica", MP, None),
        P(),
        P(),
        P("replica", MP, None, None),
        P("replica", MP, None),
        P("replica", MP),
    )
    out_specs = (P("replica", MP, None), P(MP, None), P(MP))
    return jax.shard_map(local, mesh=fine, in_specs=in_specs, out_specs=out_specs, check_vma=False)
```
